256 devices in a mesh: grid: 32 (over z, x), layer: 8 (over y, core).
Axes of the slice: x: 4, y: 4, z: 8, core: 2. Of those that a mesh axis runs over, the one named last changes fastest.
Arguments:
- a_tiles: bfloat16 [1536, 16, 128, 128], P('grid', 'layer'), may hold values from -0.5 to 0.5
- a_cols: int32 [1536, 16], P('grid', 'layer'), may hold values from 0 to 1535, as said below
- p_tiles: bfloat16 [1536, 2, 128, 128], P('grid'), may hold values from -0.5 to 0.5
- p_cols: int32 [1536, 2], P('grid'), may hold values from 0 to 31, as said below
Outputs:
- coarse: bfloat16 [32, 32, 128, 128], P('grid', 'layer')
The draws below stay inside these ranges and needn't reach their ends.
Inputs may be any that keep to these rules, and one draw needn't show every extreme that they name: `a_cols`: tile j of A lies in fine tile row j, held by grid index j // 48. Of the 48 x 2 tiles of one device, at most 6 tiles have their column on any one grid index, and exactly 6 on the device's own grid index. `p_cols`: fine tile row i, with g = i // 48, names 2 distinct coarse columns out of g - 1, g, g + 1 taken modulo 32.
All inputs are finite; a program needn't handle non-finite values.
Results may differ from the reference program's by a relative error of at most 0.0049.
Values may be sent and summed in bfloat16 or wider, within the bound.
A program may use at most 128 MiB of HBM per device.

```python
import jax
import jax.numpy as jnp
from jax import lax

B = 128
FT_DEV = 48
KL = 2
KP = 2
KA = 16
NF = 1536
NAGG = 32
CAP = 6


def draw_a_cols(key, part):
    key = jax.random.fold_in(key, 11)
    grid_count = NF // FT_DEV
    layer_count = KA // KL
    slot_total = FT_DEV * KL
    capacity = CAP
    cand_total = grid_count * capacity
    hot_owner = jax.random.randint(jax.random.fold_in(key, 1), (), 0, grid_count)
    cand_index = jnp.arange(cand_total, dtype=jnp.int32)
    peers = cand_index // capacity

    def draw_device(device_key, grid_pos):
        base_score = jax.random.randint(device_key, (cand_total,), 0, 1 << 18)
        distance = jnp.minimum((peers - grid_pos) % grid_count, (grid_pos - peers) % grid_count)
        nearness = (grid_count - distance) * (1 << 13)
        forced = jnp.where((peers == grid_pos) | (peers == hot_owner), 1 << 21, 0)
        scores = (base_score + nearness + forced) * cand_total + cand_index
        unused, chosen = lax.top_k(scores, slot_total)
        shuffled = jax.random.permutation(jax.random.fold_in(device_key, 2), slot_total)
        chosen = chosen[shuffled]
        local_rows = jax.random.randint(jax.random.fold_in(device_key, 3), (slot_total,), 0, FT_DEV)
        return chosen // capacity * FT_DEV + local_rows
    device_keys = jax.random.split(jax.random.fold_in(key, 4), grid_count * layer_count)
    grid_of_device = jnp.repeat(jnp.arange(grid_count, dtype=jnp.int32), layer_count)
    drawn = jax.vmap(draw_device)(device_keys, grid_of_device)
    drawn = drawn.reshape(grid_count, layer_count, FT_DEV, KL).transpose(0, 2, 1, 3).reshape(NF, KA)
    return drawn.astype(jnp.int32)


def draw_p_cols(key, part):
    key = jax.random.fold_in(key, 23)
    grid_count = NF // FT_DEV
    dropped = jax.random.randint(key, (NF,), 0, 3)
    swapped = jax.random.randint(jax.random.fold_in(key, 1), (NF,), 0, 2)
    grid_pos = jnp.arange(NF, dtype=jnp.int32) // FT_DEV
    first_off = jnp.where(dropped == 0, 0, -1)
    second_off = jnp.where(dropped == 2, 0, 1)
    lower = (grid_pos + first_off) % grid_count
    upper = (grid_pos + second_off) % grid_count
    left_col = jnp.where(swapped == 1, upper, lower)
    right_col = jnp.where(swapped == 1, lower, upper)
    return jnp.stack([left_col, right_col], axis=-1).astype(jnp.int32)


def level_of(own_key, extent, pieces, least, largest):
    def one(dim, blocks):
        steps = jax.random.uniform(jax.random.fold_in(jax.random.fold_in(own_key, 6), dim), (blocks,), jnp.float32, least / len(pieces), largest / len(pieces))
        return jnp.repeat(jnp.exp(steps), extent[dim] // blocks).reshape((-1,) + (1,) * (len(extent) - dim - 1))

    level = one(*pieces[0])
    for cut in pieces[1:]:
        level = level * one(*cut)
    return level


def normal_values(key, extent, spread, bound, shards=(), held_as=jnp.bfloat16):
    values = jax.random.normal(key, extent, jnp.float32) * spread
    if len(shards) > 0:
        values = level_of(key, extent, shards, -0.22, 0.18) * values
    return jnp.clip(values, min=-bound, max=bound).astype(held_as)


def setup_inputs(seed: int = 0) -> dict:
    key_of = jax.random.split(jax.random.key(seed), 5)
    a_tiles = normal_values(key_of[0], (NF, KA, B, B), B ** -0.5, 0.5, ((0, 32), (1, 8)))
    a_cols = draw_a_cols(jax.random.fold_in(key_of[4], 71), 0)
    p_tiles = normal_values(key_of[2], (NF, KP, B, B), B ** -0.5, 0.5, ((0, 32),))
    p_cols = draw_p_cols(jax.random.fold_in(key_of[4], 71), 0)
    return {"a_tiles": a_tiles, "a_cols": a_cols, "p_tiles": p_tiles, "p_cols": p_cols}


def reference(a_tiles, a_cols, p_tiles, p_cols):
    fine_total = a_tiles.shape[0]
    accumulated = jnp.zeros((NAGG, NAGG, B, B), jnp.float32)

    def per_row(carry, row_index):
        a_row = lax.dynamic_index_in_dim(a_tiles, row_index, 0, False)
        col_row = lax.dynamic_index_in_dim(a_cols, row_index, 0, False)
        p_row = lax.dynamic_index_in_dim(p_tiles, row_index, 0, False)
        pcol_row = lax.dynamic_index_in_dim(p_cols, row_index, 0, False)
        fetched = p_tiles[col_row]
        fetched_cols = p_cols[col_row]
        product = jnp.einsum('kab,ktbc->ktac', a_row.astype(jnp.float32), fetched.astype(jnp.float32)).astype(jnp.bfloat16)
        triple = jnp.einsum('sba,ktbc->kstac', p_row.astype(jnp.float32), product.astype(jnp.float32))
        row_ids = jnp.broadcast_to(pcol_row[None, :, None], (KA, KP, KP)).astype(jnp.int32)
        col_ids = jnp.broadcast_to(fetched_cols[:, None, :], (KA, KP, KP)).astype(jnp.int32)
        carry = carry.at[row_ids, col_ids].add(triple)
        return carry, None

    accumulated, unused = lax.scan(per_row, accumulated, jnp.arange(fine_total, dtype=jnp.int32))
    return accumulated.astype(jnp.bfloat16)
```

```python
import functools

import jax
import jax.numpy as jnp
from jax import lax
from jax.experimental import pallas as pl
from jax.experimental.pallas import tpu as pltpu
from jax.sharding import PartitionSpec as P

MESH = pl.DeviceIdType.MESH
SHIFT = 64
CHUNK = 4
LAG = 2


def bucket_kernel(cap, fine_rows, per_layer, a_cols, perm, meta):
    layers, owner_slots = meta.shape[0], perm.shape[0]
    owners = owner_slots // cap
    per = owners // layers * cap

    def clear(s, unused):
        perm[s] = 0
        meta[s // per, 0, s % per] = fine_rows * SHIFT
        return unused

    lax.fori_loop(0, owner_slots, clear, 0)

    def scoped(count):
        def zero(g, unused):
            count[g] = 0
            return unused

        lax.fori_loop(0, owners, zero, 0)

        def place(r, unused):
            for k in range(per_layer):
                col = a_cols[r, k]
                owner = col // fine_rows
                at = owner * cap + count[owner]
                count[owner] = count[owner] + 1
                perm[at] = r * per_layer + k
                meta[at // per, 0, at % per] = r * SHIFT + (col - owner * fine_rows)
            return unused

        lax.fori_loop(0, fine_rows, place, 0)

    pl.run_scoped(scoped, pltpu.SMEM((owners,), jnp.int32))


def main_kernel(
    nz, nx, nl, cap,
    perm, pc_s, a_hbm, p_hbm, meta_v, pc_v, out_ref,
    a_vm, p_own, asend, arecv, metar, meta_s, pbuf, pcbuf, pcs, ptw, wide, tot, hsend_i, hsend_c, hrecv_i, hrecv_c,
    load_sem, as_sem, ar_sem, ms_sem, mr_sem, zs, zr, xs, xr, fs, fr, pcss, pcr, hs, hr,
):
    fine = p_own.shape[0]
    half = fine // 2
    chunks = half // CHUNK
    nq = nx
    layer = lax.axis_index("layer")
    grid = lax.axis_index("grid")
    z, x = grid // nx, grid % nx
    d = lax.rem(z - layer + nz, nz)
    up = lax.rem(z + 1, nz) * nx + x
    down = lax.rem(z + nz - 1, nz) * nx + x
    right = z * nx + lax.rem(x + 1, nx)
    left = z * nx + lax.rem(x + nx - 1, nx)
    after, before = lax.rem(grid + 1, nz * nx), lax.rem(grid + nz * nx - 1, nz * nx)
    lafter, lbefore = lax.rem(layer + 1, nl), lax.rem(layer + nl - 1, nl)

    def remote(src, dst, ssem, rsem, g, l):
        return pltpu.make_async_remote_copy(
            src_ref=src, dst_ref=dst, send_sem=ssem, recv_sem=rsem, device_id=(g, l), device_id_type=MESH
        )

    load_a = pltpu.make_async_copy(a_hbm, a_vm, load_sem.at[0])
    load_p = pltpu.make_async_copy(p_hbm, p_own, load_sem.at[1])
    load_p.start()
    load_a.start()

    @pl.when(d == 0)
    def _():
        first = pltpu.make_async_copy(p_hbm, pbuf.at[0], load_sem.at[2])
        first.start()
        first.wait()
        cols = pltpu.make_async_copy(pc_v, pcbuf.at[0], load_sem.at[2])
        cols.start()
        cols.wait()

    barrier = pltpu.get_barrier_semaphore()
    partners = [(up, layer), (down, layer), (right, layer), (left, layer)]
    partners += [(grid, lax.rem(layer + k, nl)) for k in range(1, nl)]
    partners += [(g, l) for g in (after, before) for l in (layer, lafter, lbefore)]
    for g, l in partners:
        pl.semaphore_signal(barrier, inc=1, device_id=(g, l), device_id_type=MESH)
    pl.semaphore_wait(barrier, len(partners))

    load_a.wait()

    per = nq * cap

    def bucket(to):
        def one(s, unused):
            g = to * nq + s // cap
            asend[g, s % cap] = a_vm[perm[to * per + s]]
            return unused

        lax.fori_loop(0, per, one, 0)

    def a_copy(k):
        to = lax.rem(layer + k, nl)
        return remote(asend.at[pl.ds(to * nq, nq)], arecv.at[layer], as_sem.at[k], ar_sem.at[k], grid, to)

    def m_copy(k):
        to = lax.rem(layer + k, nl)
        return remote(meta_v.at[to], metar.at[layer], ms_sem.at[k], mr_sem.at[k], grid, to)

    def send_a(k, unused):
        to = lax.rem(layer + k, nl)
        bucket(to)
        a_copy(k).start()
        m_copy(k).start()
        return unused

    lax.fori_loop(1, nl, send_a, 0)
    bucket(layer)
    own_a = pltpu.make_async_copy(asend.at[pl.ds(layer * nq, nq)], arecv.at[layer], load_sem.at[2])
    own_a.start()
    own_m = pltpu.make_async_copy(meta_v.at[layer], metar.at[layer], load_sem.at[3])
    own_m.start()
    load_p.wait()

    def block(rel, s, c):
        return pbuf.at[rel, pl.ds(s * half + c * CHUNK, CHUNK)]

    def z_copy(s, c):
        blk = block(0, s, c)
        return remote(blk, blk, zs.at[s, c], zr.at[s, c], (up, down)[s], layer)

    def x_copy(side, s, c):
        return remote(
            block(0, s, c), block((3, 1)[side], s, c), xs.at[side, s, c], xr.at[side, s, c], (right, left)[side], layer
        )

    def f_copy(s, c):
        return remote(block((3, 1)[s], s, c), block(2, s, c), fs.at[s, c], fr.at[s, c], (right, left)[s], layer)

    def pc_copy(which):
        src, dst, g = ((0, 0, up), (0, 3, right), (0, 1, left), (3, 2, right))[which]
        return remote(pcbuf.at[src], pcbuf.at[dst], pcss.at[which], pcr.at[which], g, layer)

    def transpose_rows(lo):
        for r in range(4):
            i = lo * 4 + r
            o0 = lax.rem(pc_s[i, 0] - grid + 1 + nz * nx, nz * nx)
            o1 = lax.rem(pc_s[i, 1] - grid + 1 + nz * nx, nz * nx)
            t0 = p_own[i, 0].T
            t1 = p_own[i, 1].T
            zero = jnp.zeros_like(t0)
            for b in range(3):
                ptw[i, b * 128 : (b + 1) * 128, :] = jnp.where(o0 == b, t0, jnp.where(o1 == b, t1, zero))

    ptw[fine] = jnp.zeros(ptw.shape[1:], ptw.dtype)

    steps = chunks + nz + LAG

    def step(t, unused):
        for s in (0, 1):
            hop = d if s == 0 else lax.rem(nz - d, nz)
            c = t - hop

            @pl.when((c >= 0) & (c < chunks))
            def _():
                @pl.when(d != 0)
                def _():
                    z_copy(s, c).wait_recv()

                @pl.when(hop < nz - 1)
                def _():
                    z_copy(s, c).start()

                x_copy(0, s, c).start()
                x_copy(1, s, c).start()
                if s == 0:

                    @pl.when(c == 0)
                    def _():
                        @pl.when(d != 0)
                        def _():
                            pc_copy(0).wait_recv()

                        @pl.when(hop < nz - 1)
                        def _():
                            pc_copy(0).start()

                        pc_copy(1).start()
                        pc_copy(2).start()

            f = c - LAG

            @pl.when((f >= 0) & (f < chunks))
            def _():
                x_copy(s, s, f).wait_recv()
                f_copy(s, f).start()
                if s == 0:

                    @pl.when(f == 0)
                    def _():
                        pc_copy(1).wait_recv()
                        pc_copy(3).start()

        @pl.when(t < fine // 4)
        def _():
            transpose_rows(t)

        return unused

    lax.fori_loop(0, max(steps, fine // 4), step, 0)

    def a_wait(k, unused):
        a_copy(k).wait_recv()
        m_copy(k).wait_recv()
        return unused

    lax.fori_loop(1, nl, a_wait, 0)
    own_a.wait()
    own_m.wait()
    pc_copy(2).wait_recv()
    pc_copy(3).wait_recv()
    tables = pltpu.make_async_copy(metar, meta_s, load_sem.at[2])
    tables.start()
    tables.wait()
    tables = pltpu.make_async_copy(pcbuf, pcs, load_sem.at[2])
    tables.start()
    tables.wait()

    tot[...] = jnp.zeros_like(tot)
    slots = nl * cap
    group = 4

    def accumulate(rel):
        q = lax.rem(x + rel, nx)
        owner = layer * nq + q

        def widen(j, unused):
            o0 = lax.rem(pcs[rel, 0, 2 * j] - owner + 1 + nz * nx, nz * nx)
            o1 = lax.rem(pcs[rel, 0, 2 * j + 1] - owner + 1 + nz * nx, nz * nx)
            t0 = pbuf[rel, j, 0]
            t1 = pbuf[rel, j, 1]
            zero = jnp.zeros_like(t0)
            for b in range(3):
                wide[j, :, b * 128 : (b + 1) * 128] = jnp.where(o0 == b, t0, jnp.where(o1 == b, t1, zero))
            return unused

        lax.fori_loop(0, fine, widen, 0)

        def some(u, acc):
            lefts, prods = [], []
            for v in range(group):
                n = u * group + v
                src, k = n // cap, n % cap
                m = meta_s[src, 0, q * cap + k]
                i, j = m // SHIFT, m % SHIFT
                prods.append(
                    jnp.dot(arecv[src, q, k], wide[j], preferred_element_type=jnp.float32).astype(jnp.bfloat16)
                )
                lefts.append(ptw[i])
            return acc + jnp.dot(
                jnp.concatenate(lefts, axis=1), jnp.concatenate(prods, axis=0), preferred_element_type=jnp.float32
            )

        acc = lax.fori_loop(0, slots // group, some, jnp.zeros((384, 384), jnp.float32))
        for a in range(3):
            for b in range(3):
                tot[a, q + b] += acc[a * 128 : (a + 1) * 128, b * 128 : (b + 1) * 128]

    accumulate(0)

    def wait_rest(side):
        def one(c, unused):
            x_copy(side, 1 - side, c).wait_recv()
            return unused

        lax.fori_loop(0, chunks, one, 0)

    wait_rest(0)
    accumulate(3)
    wait_rest(1)
    accumulate(1)

    def wait_forward(c, unused):
        f_copy(0, c).wait_recv()
        f_copy(1, c).wait_recv()
        return unused

    lax.fori_loop(0, chunks, wait_forward, 0)
    accumulate(2)

    bf = jnp.bfloat16
    hsend_i[0] = tot[2, 1 : nq + 1].astype(bf)
    hsend_i[1] = tot[0, 1 : nq + 1].astype(bf)
    hsend_c[0] = tot[1, nq + 1].astype(bf)
    hsend_c[1] = tot[1, 0].astype(bf)
    hsend_c[2] = tot[2, nq + 1].astype(bf)
    hsend_c[3] = tot[2, 0].astype(bf)
    hsend_c[4] = tot[0, nq + 1].astype(bf)
    hsend_c[5] = tot[0, 0].astype(bf)
    copies = [
        remote(hsend_i.at[k], hrecv_i.at[k], hs.at[k], hr.at[k], g, layer) for k, g in enumerate((after, before))
    ]
    to = [(g, l) for g in (grid, after, before) for l in (lafter, lbefore)]
    copies += [
        remote(hsend_c.at[k], hrecv_c.at[k], hs.at[2 + k], hr.at[2 + k], g, l) for k, (g, l) in enumerate(to)
    ]
    for copy in copies:
        copy.start()
    for copy in copies:
        copy.wait_recv()
    for b in range(nq):
        total = tot[1, 1 + b]
        for k in range(2):
            total = total + hrecv_i[k, b].astype(jnp.float32)
        if b == 0:
            for k in (0, 2, 4):
                total = total + hrecv_c[k].astype(jnp.float32)
        if b == nq - 1:
            for k in (1, 3, 5):
                total = total + hrecv_c[k].astype(jnp.float32)
        out_ref[0, b] = total.astype(bf)

    for copy in copies:
        copy.wait_send()

    def a_sent(k, unused):
        a_copy(k).wait_send()
        m_copy(k).wait_send()
        return unused

    lax.fori_loop(1, nl, a_sent, 0)

    def sent(c, unused):
        for s in (0, 1):
            hop = d if s == 0 else lax.rem(nz - d, nz)

            @pl.when(hop < nz - 1)
            def _():
                z_copy(s, c).wait_send()

            x_copy(0, s, c).wait_send()
            x_copy(1, s, c).wait_send()
            f_copy(s, c).wait_send()
        return unused

    lax.fori_loop(0, chunks, sent, 0)

    @pl.when(d < nz - 1)
    def _():
        pc_copy(0).wait_send()

    for which in (1, 2, 3):
        pc_copy(which).wait_send()


def local(nx, a_tiles, a_cols, p_tiles, p_cols):
    fine, per_layer, size, unused = a_tiles.shape
    nl, ng = lax.axis_size("layer"), lax.axis_size("grid")
    nz = ng // nx
    cap = 2 * fine * per_layer // ng
    smem = pl.BlockSpec(memory_space=pltpu.SMEM)
    anywhere = pl.BlockSpec(memory_space=pl.ANY)
    perm, meta = pl.pallas_call(
        functools.partial(bucket_kernel, cap, fine, per_layer),
        out_shape=(
            jax.ShapeDtypeStruct((ng * cap,), jnp.int32),
            jax.ShapeDtypeStruct((nl, 1, 128), jnp.int32),
        ),
        in_specs=[smem],
        out_specs=(smem, smem),
    )(a_cols)
    pc_flat = jnp.pad(p_cols.reshape(1, -1), ((0, 0), (0, 128 - 2 * fine)))
    chunks = fine // 2 // CHUNK
    bf, f32, i32 = jnp.bfloat16, jnp.float32, jnp.int32
    dma = pltpu.SemaphoreType.DMA
    return pl.pallas_call(
        functools.partial(main_kernel, nz, nx, nl, cap),
        out_shape=jax.ShapeDtypeStruct((1, nx, size, size), bf),
        in_specs=[smem, smem, anywhere, anywhere, anywhere, anywhere],
        out_specs=pl.BlockSpec(memory_space=pltpu.VMEM),
        scratch_shapes=[
            pltpu.VMEM((fine * per_layer, size, size), bf),
            pltpu.VMEM(p_tiles.shape, bf),
            pltpu.VMEM((ng, cap, size, size), bf),
            pltpu.VMEM((nl, nx, cap, size, size), bf),
            pltpu.VMEM((nl, 1, 128), i32),
            pltpu.SMEM((nl, 1, 128), i32),
            pltpu.VMEM((nx,) + p_tiles.shape, bf),
            pltpu.VMEM((nx, 1, 128), i32),
            pltpu.SMEM((nx, 1, 128), i32),
            pltpu.VMEM((fine + 1, 3 * size, size), bf),
            pltpu.VMEM((fine, size, 3 * size), bf),
            pltpu.VMEM((3, nx + 2, size, size), f32),
            pltpu.VMEM((2, nx, size, size), bf),
            pltpu.VMEM((6, size, size), bf),
            pltpu.VMEM((2, nx, size, size), bf),
            pltpu.VMEM((6, size, size), bf),
            dma((4,)),
            dma((nl,)), dma((nl,)), dma((nl,)), dma((nl,)),
            dma((2, chunks)), dma((2, chunks)),
            dma((2, 2, chunks)), dma((2, 2, chunks)),
            dma((2, chunks)), dma((2, chunks)),
            dma((4,)), dma((4,)),
            dma((8,)), dma((8,)),
        ],
        compiler_params=pltpu.CompilerParams(
            collective_id=0, has_side_effects=True, vmem_limit_bytes=56 * 1024 * 1024
        ),
    )(perm, p_cols, a_tiles.reshape(fine * per_layer, size, size), p_tiles, meta, pc_flat)


def solution(mesh):
    nx = 4
    return jax.shard_map(
        functools.partial(local, nx),
        mesh=mesh,
        in_specs=(
            P("grid", "layer", None, None),
            P("grid", "layer"),
            P("grid", None, None, None),
            P("grid", None),
        ),
        out_specs=P("grid", "layer", None, None),
        check_vma=False,
    )
```

```python
import functools

import jax
import jax.numpy as jnp
from jax import lax
from jax.experimental import pallas as pl
from jax.experimental.pallas import tpu as pltpu
from jax.sharding import PartitionSpec as P

MESH = pl.DeviceIdType.MESH
SHIFT = 64
CHUNK = 1
LAG = 3
PASS = 0
PLANE_ROWS = 16
HOP = 3
GROUP = 8
WIDEN = 12


def main_kernel(
    nz, nx, nl, cap, per_layer,
    tab, a_hbm, p_hbm, out_ref,
    tabv, tabs, permv, perms, a_vm, p_own, asend, arecv, metav, metar, meta_s, pbuf, pcbuf, pcs, ptw, wide, acc, tot,
    hsend_i, hsend_c, hrecv_i, hrecv_c,
    load_sem, as_sem, ar_sem, ms_sem, mr_sem, zs, zr, xs, xr, fs, fr, rs, rr, gs, gr, pcss, pcr, hs, hr,
):
    fine = p_own.shape[0]
    half = fine // 2
    late = PLANE_ROWS // 2
    early = half - late
    early_chunks, late_chunks = early // CHUNK, late // CHUNK
    chunks = early_chunks + nx * late_chunks
    ng = nz * nx
    layer = lax.axis_index("layer")
    grid = lax.axis_index("grid")
    z, x = grid // nx, grid % nx
    d = lax.rem(z - layer + nz, nz)
    up = lax.rem(z + 1, nz) * nx + x
    down = lax.rem(z + nz - 1, nz) * nx + x
    right = z * nx + lax.rem(x + 1, nx)
    left = z * nx + lax.rem(x + nx - 1, nx)
    after, before = lax.rem(grid + 1, ng), lax.rem(grid + ng - 1, ng)
    lafter, lbefore = lax.rem(layer + 1, nl), lax.rem(layer + nl - 1, nl)

    def remote(src, dst, ssem, rsem, g, l):
        return pltpu.make_async_remote_copy(
            src_ref=src, dst_ref=dst, send_sem=ssem, recv_sem=rsem, device_id=(g, l), device_id_type=MESH
        )

    def turn(o):
        return o + o // 2 * (1 - 2 * (o % 2))

    load_p = pltpu.make_async_copy(p_hbm, p_own, load_sem.at[1])
    load_a = pltpu.make_async_copy(a_hbm, a_vm, load_sem.at[0])
    load_t = pltpu.make_async_copy(tab, tabv, load_sem.at[2])
    load_s = pltpu.make_async_copy(tab, tabs, load_sem.at[3])
    first = pltpu.make_async_copy(p_hbm, pbuf.at[0], load_sem.at[4])
    cols = pltpu.make_async_copy(tab.at[2], pcbuf.at[0], load_sem.at[5])

    @pl.when(d == 0)
    def _():
        first.start()
        cols.start()

    load_t.start()
    load_s.start()
    load_a.start()
    load_p.start()

    barrier = pltpu.get_barrier_semaphore()
    partners = [(up, layer), (down, layer), (right, layer), (left, layer)]
    partners += [(grid, lax.rem(layer + k, nl)) for k in range(1, nl)]
    partners += [(g, l) for g in (after, before) for l in (layer, lafter, lbefore)]
    for g, l in partners:
        pl.semaphore_signal(barrier, inc=1, device_id=(g, l), device_id_type=MESH)
    pl.semaphore_wait(barrier, len(partners))

    @pl.when(d == 0)
    def _():
        first.wait()
        cols.wait()

    def early_block(rel, s, c):
        return pbuf.at[rel, pl.ds(s * half + c * CHUNK, CHUNK)]

    def late_block(rel, s):
        return pbuf.at[rel, pl.ds(s * half + early, late)]

    def z_copy(s, c):
        e = jnp.maximum(c - early_chunks, 0)
        is_late = jnp.minimum(jnp.maximum(c - early_chunks + 1, 0), 1)
        rel = turn(e // late_chunks)
        row = s * half + is_late * (early + e % late_chunks * CHUNK) + (1 - is_late) * c * CHUNK
        blk = pbuf.at[rel, pl.ds(row, CHUNK)]
        return remote(blk, blk, zs.at[s, c], zr.at[s, c], (up, down)[s], layer)

    def x_copy(side, s, c):
        return remote(
            early_block(0, s, c), early_block((3, 1)[side], s, c), xs.at[side, s, c], xr.at[side, s, c],
            (right, left)[side], layer,
        )

    def f_copy(s, c):
        return remote(
            early_block((3, 1)[s], s, c), early_block(2, s, c), fs.at[s, c], fr.at[s, c], (right, left)[s], layer
        )

    def r_copy(side, s):
        return remote(
            late_block(0, s), late_block((3, 1)[side], s), rs.at[side, s], rr.at[side, s], (right, left)[side], layer
        )

    def g_copy(s):
        return remote(late_block((3, 1)[s], s), late_block(2, s), gs.at[s], gr.at[s], (right, left)[s], layer)

    def pc_copy(which):
        src, dst, g = ((0, 0, up), (0, 3, right), (0, 1, left), (3, 2, right))[which]
        return remote(pcbuf.at[src], pcbuf.at[dst], pcss.at[which], pcr.at[which], g, layer)

    hops = (d, lax.rem(nz - d, nz))
    near, far = jnp.minimum(*hops), jnp.maximum(*hops)
    near_turn = HOP * near
    far_turn = jnp.maximum(near_turn + early_chunks, HOP * far)
    up_first = jnp.minimum(jnp.maximum(hops[1] - hops[0] + 1, 0), 1)
    x_turn = (
        up_first * near_turn + (1 - up_first) * far_turn,
        up_first * far_turn + (1 - up_first) * near_turn,
    )
    pass_turn = jnp.maximum(far_turn + early_chunks + LAG, chunks + PASS)
    ready = jnp.maximum(early_chunks + late_chunks + HOP * far, pass_turn + early_chunks - late_chunks)

    def p_step(t):
        for s in (0, 1):
            hop = hops[s]
            c = t - HOP * hop

            @pl.when((c >= 0) & (c < chunks))
            def _():
                @pl.when(d != 0)
                def _():
                    z_copy(s, c).wait_recv()

                @pl.when(d == 0)
                def _():
                    @pl.when(c == early_chunks + (1 + s) * late_chunks)
                    def _():
                        r_copy(1 - s, s).wait_recv()

                    @pl.when(c == early_chunks + 3 * late_chunks)
                    def _():
                        g_copy(s).wait_recv()

                @pl.when(hop < nz - 1)
                def _():
                    z_copy(s, c).start()

                if s == 0:

                    @pl.when(c == 0)
                    def _():
                        @pl.when(d != 0)
                        def _():
                            pc_copy(0).wait_recv()

                        @pl.when(hop < nz - 1)
                        def _():
                            pc_copy(0).start()

                        pc_copy(1).start()
                        pc_copy(2).start()

                    @pl.when(c == 2)
                    def _():
                        pc_copy(1).wait_recv()
                        pc_copy(3).start()

                @pl.when((d == 0) & (c == 0))
                def _():
                    r_copy(0, s).start()
                    r_copy(1, s).start()

                @pl.when((d == 0) & (c == early_chunks))
                def _():
                    r_copy(s, s).wait_recv()
                    g_copy(s).start()

            e = t - x_turn[s]

            @pl.when((e >= 0) & (e < early_chunks))
            def _():
                x_copy(0, s, e).start()
                x_copy(1, s, e).start()

        f = t - pass_turn

        @pl.when((f >= 0) & (f < early_chunks))
        def _():
            for s in (0, 1):
                x_copy(s, s, f).wait_recv()
                f_copy(s, f).start()

    p_step(0)

    load_t.wait()
    size = tabv.shape[2]
    per = nx * cap
    blank = fine * SHIFT
    rows = lax.broadcasted_iota(jnp.int32, (size, size), 0)
    lanes = lax.broadcasted_iota(jnp.int32, (size, size), 1)

    def upright(v):
        return jnp.broadcast_to(v, (size, size)).T

    own = tabv[0]
    same = (upright(own) == jnp.broadcast_to(own, (size, size))) & (rows < lanes)
    rank = jnp.sum(jnp.where(same, 1, 0), axis=0, keepdims=True)
    slot = upright(own * cap + rank)
    value = upright(tabv[1] - blank)
    for l in range(nl):
        hit = (slot == l * per + lanes) & (lanes < per) & (rows < a_vm.shape[0])
        permv[l] = jnp.sum(jnp.where(hit, rows, 0), axis=0, keepdims=True)
        metav[l] = blank + jnp.sum(jnp.where(hit, value, 0), axis=0, keepdims=True)
    to_smem = pltpu.make_async_copy(permv, perms, load_sem.at[6])
    to_smem.start()

    def m_copy(k):
        to = lax.rem(layer + k, nl)
        return remote(metav.at[to], metar.at[layer], ms_sem.at[k], mr_sem.at[k], grid, to)

    def send_m(k, unused):
        m_copy(k).start()
        return unused

    lax.fori_loop(1, nl, send_m, 0)
    metar[layer] = metav[layer]
    to_smem.wait()
    load_a.wait()

    def a_copy(o, k):
        to = lax.rem(layer + k, nl)
        q = lax.rem(x + turn(o), nx)
        return remote(asend.at[to * nx + q], arecv.at[layer, q], as_sem.at[o, k], ar_sem.at[o, k], grid, to)

    def a_phase(o):
        q = lax.rem(x + turn(o), nx)

        def send_a(k, unused):
            to = lax.rem(layer + k, nl)
            for c in range(cap):
                asend[to * nx + q, c] = a_vm[perms[to, 0, q * cap + c]]
            a_copy(o, k).start()
            return unused

        lax.fori_loop(1, nl, send_a, 0)
        for c in range(cap):
            arecv[layer, q, c] = a_vm[perms[layer, 0, q * cap + c]]

    a_phase(0)
    load_p.wait()
    load_s.wait()
    ptw[fine] = jnp.zeros(ptw.shape[1:], ptw.dtype)
    tot[...] = jnp.zeros_like(tot)

    def spread(ref, at, o0, o1, t0, t1, upright_blocks):
        zero = jnp.zeros_like(t0)
        for b in range(3):
            tile = jnp.where(o0 == b, t0, jnp.where(o1 == b, t1, zero))
            if upright_blocks:
                ref[at, b * 128 : (b + 1) * 128, :] = tile
            else:
                ref[at, :, b * 128 : (b + 1) * 128] = tile

    def offset(col, g):
        return lax.rem(col - g + 1 + ng, ng)

    def transpose_rows(lo):
        for r in range(4):
            i = lo * 4 + r
            o0, o1 = offset(tabs[2, 0, 2 * i], grid), offset(tabs[2, 0, 2 * i + 1], grid)
            spread(ptw, i, o0, o1, p_own[i, 0].T, p_own[i, 1].T, True)

    slots = nl * cap
    widen_units, group_units = fine // WIDEN, slots // GROUP
    units = widen_units + group_units

    def arrive(o):
        rel = turn(o)

        def a_wait(k, unused):
            a_copy(o, k).wait_recv()
            return unused

        lax.fori_loop(1, nl, a_wait, 0)

        @pl.when(o == 0)
        def _():
            def m_wait(k, unused):
                m_copy(k).wait_recv()
                return unused

            lax.fori_loop(1, nl, m_wait, 0)
            pc_copy(2).wait_recv()
            pc_copy(3).wait_recv()
            tables = pltpu.make_async_copy(metar, meta_s, load_sem.at[2])
            tables.start()
            columns = pltpu.make_async_copy(pcbuf, pcs, load_sem.at[3])
            columns.start()
            tables.wait()
            columns.wait()

        for side, at in ((1, 1), (0, 2)):

            @pl.when(o == at)
            def _():
                def one(c, unused):
                    x_copy(side, 1 - side, c).wait_recv()
                    return unused

                lax.fori_loop(0, early_chunks, one, 0)

        @pl.when(o == 3)
        def _():
            def one(c, unused):
                f_copy(0, c).wait_recv()
                f_copy(1, c).wait_recv()
                return unused

            lax.fori_loop(0, early_chunks, one, 0)

    def widen(rel, lo):
        owner = layer * nx + lax.rem(x + rel, nx)

        def one(r, unused):
            j = lo * WIDEN + r
            o0, o1 = offset(pcs[rel, 0, 2 * j], owner), offset(pcs[rel, 0, 2 * j + 1], owner)
            spread(wide, j, o0, o1, pbuf[rel, j, 0], pbuf[rel, j, 1], False)
            return unused

        lax.fori_loop(0, WIDEN, one, 0)

    def some(rel, u):
        q = lax.rem(x + rel, nx)
        lefts, prods = [], []
        for v in range(GROUP):
            n = u * GROUP + v
            src, k = n // cap, n % cap
            m = meta_s[src, 0, q * cap + k]
            i, j = m // SHIFT, m % SHIFT
            prods.append(jnp.dot(arecv[src, q, k], wide[j], preferred_element_type=jnp.float32).astype(jnp.bfloat16))
            lefts.append(ptw[i])
        acc[...] += jnp.dot(
            jnp.concatenate(lefts, axis=1), jnp.concatenate(prods, axis=0), preferred_element_type=jnp.float32
        )

    def flush(rel):
        q = lax.rem(x + rel, nx)
        for a in range(3):
            for b in range(3):
                tot[a, q + b] += acc[a * 128 : (a + 1) * 128, b * 128 : (b + 1) * 128]

    def unit(n):
        o, w = n // units, n % units
        rel = turn(o)

        @pl.when(w == 0)
        def _():
            arrive(o)

        @pl.when(w < widen_units)
        def _():
            widen(rel, w)

        @pl.when(w == widen_units)
        def _():
            acc[...] = jnp.zeros_like(acc)

        @pl.when(w >= widen_units)
        def _():
            some(rel, w - widen_units)

        @pl.when(w == units - 1)
        def _():
            flush(rel)

    pace = -(-units // late_chunks)

    def step(t, unused):
        p_step(t)

        @pl.when(t < nx)
        def _():
            a_phase(t)

        @pl.when(t <= fine // 4)
        def _():
            transpose_rows(t - 1)

        @pl.when(t >= ready)
        def _():
            o, at = (t - ready) // late_chunks, (t - ready) % late_chunks

            def one(v, unused):
                w = at * pace + v

                @pl.when(w < units)
                def _():
                    unit(o * units + w)

                return unused

            lax.fori_loop(0, pace, one, 0)

        return unused

    lax.fori_loop(1, ready + nx * late_chunks, step, 0)

    bf = jnp.bfloat16
    hsend_i[0] = tot[2, 1 : nx + 1].astype(bf)
    hsend_i[1] = tot[0, 1 : nx + 1].astype(bf)
    hsend_c[0] = tot[1, nx + 1].astype(bf)
    hsend_c[1] = tot[1, 0].astype(bf)
    hsend_c[2] = tot[2, nx + 1].astype(bf)
    hsend_c[3] = tot[2, 0].astype(bf)
    hsend_c[4] = tot[0, nx + 1].astype(bf)
    hsend_c[5] = tot[0, 0].astype(bf)
    copies = [
        remote(hsend_i.at[k], hrecv_i.at[k], hs.at[k], hr.at[k], g, layer) for k, g in enumerate((after, before))
    ]
    to = [(g, l) for g in (grid, after, before) for l in (lafter, lbefore)]
    copies += [
        remote(hsend_c.at[k], hrecv_c.at[k], hs.at[2 + k], hr.at[2 + k], g, l) for k, (g, l) in enumerate(to)
    ]
    for copy in copies:
        copy.start()
    for copy in copies:
        copy.wait_recv()
    for b in range(nx):
        total = tot[1, 1 + b]
        for k in range(2):
            total = total + hrecv_i[k, b].astype(jnp.float32)
        if b == 0:
            for k in (0, 2, 4):
                total = total + hrecv_c[k].astype(jnp.float32)
        if b == nx - 1:
            for k in (1, 3, 5):
                total = total + hrecv_c[k].astype(jnp.float32)
        out_ref[0, b] = total.astype(bf)

    for copy in copies:
        copy.wait_send()

    def a_sent(k, unused):
        for o in range(nx):
            a_copy(o, k).wait_send()
        m_copy(k).wait_send()
        return unused

    lax.fori_loop(1, nl, a_sent, 0)

    for s in (0, 1):
        hop = d if s == 0 else lax.rem(nz - d, nz)

        def z_sent(c, unused):
            z_copy(s, c).wait_send()
            return unused

        @pl.when(hop < nz - 1)
        def _():
            lax.fori_loop(0, chunks, z_sent, 0)

        def x_sent(c, unused):
            x_copy(0, s, c).wait_send()
            x_copy(1, s, c).wait_send()
            f_copy(s, c).wait_send()
            return unused

        lax.fori_loop(0, early_chunks, x_sent, 0)

    @pl.when(d < nz - 1)
    def _():
        pc_copy(0).wait_send()

    @pl.when(d == 0)
    def _():
        for s in (0, 1):
            r_copy(0, s).wait_send()
            r_copy(1, s).wait_send()
            g_copy(s).wait_send()

    for which in (1, 2, 3):
        pc_copy(which).wait_send()


def local(nx, a_tiles, a_cols, p_tiles, p_cols):
    fine, per_layer, size, unused = a_tiles.shape
    nl, ng = lax.axis_size("layer"), lax.axis_size("grid")
    nz = ng // nx
    slot_total = fine * per_layer
    cap = 2 * slot_total // ng
    anywhere = pl.BlockSpec(memory_space=pl.ANY)
    flat = a_cols.reshape(1, slot_total)
    rows = lax.broadcasted_iota(jnp.int32, (1, slot_total), 1) // per_layer
    tab = jnp.stack(
        [
            jnp.pad(flat // fine, ((0, 0), (0, 128 - slot_total)), constant_values=4096),
            jnp.pad(rows * SHIFT + flat % fine, ((0, 0), (0, 128 - slot_total))),
            jnp.pad(p_cols.reshape(1, -1), ((0, 0), (0, 128 - 2 * fine))),
        ]
    )
    half = fine // 2
    early_chunks = (half - PLANE_ROWS // 2) // CHUNK
    chunks = early_chunks + nx * (PLANE_ROWS // 2 // CHUNK)
    bf, f32, i32 = jnp.bfloat16, jnp.float32, jnp.int32
    dma = pltpu.SemaphoreType.DMA
    return pl.pallas_call(
        functools.partial(main_kernel, nz, nx, nl, cap, per_layer),
        out_shape=jax.ShapeDtypeStruct((1, nx, size, size), bf),
        in_specs=[anywhere, anywhere, anywhere],
        out_specs=pl.BlockSpec(memory_space=pltpu.VMEM),
        scratch_shapes=[
            pltpu.VMEM((3, 1, 128), i32),
            pltpu.SMEM((3, 1, 128), i32),
            pltpu.VMEM((nl, 1, 128), i32),
            pltpu.SMEM((nl, 1, 128), i32),
            pltpu.VMEM((slot_total, size, size), bf),
            pltpu.VMEM(p_tiles.shape, bf),
            pltpu.VMEM((ng, cap, size, size), bf),
            pltpu.VMEM((nl, nx, cap, size, size), bf),
            pltpu.VMEM((nl, 1, 128), i32),
            pltpu.VMEM((nl, 1, 128), i32),
            pltpu.SMEM((nl, 1, 128), i32),
            pltpu.VMEM((nx,) + p_tiles.shape, bf),
            pltpu.VMEM((nx, 1, 128), i32),
            pltpu.SMEM((nx, 1, 128), i32),
            pltpu.VMEM((fine + 1, 3 * size, size), bf),
            pltpu.VMEM((fine, size, 3 * size), bf),
            pltpu.VMEM((3 * size, 3 * size), f32),
            pltpu.VMEM((3, nx + 2, size, size), f32),
            pltpu.VMEM((2, nx, size, size), bf),
            pltpu.VMEM((6, size, size), bf),
            pltpu.VMEM((2, nx, size, size), bf),
            pltpu.VMEM((6, size, size), bf),
            dma((7,)),
            dma((nx, nl)), dma((nx, nl)), dma((nl,)), dma((nl,)),
            dma((2, chunks)), dma((2, chunks)),
            dma((2, 2, early_chunks)), dma((2, 2, early_chunks)),
            dma((2, early_chunks)), dma((2, early_chunks)),
            dma((2, 2)), dma((2, 2)), dma((2,)), dma((2,)),
            dma((4,)), dma((4,)),
            dma((8,)), dma((8,)),
        ],
        compiler_params=pltpu.CompilerParams(
            collective_id=0, has_side_effects=True, vmem_limit_bytes=58 * 1024 * 1024
        ),
    )(tab, a_tiles.reshape(slot_total, size, size), p_tiles)


def solution(mesh):
    nx = 4
    return jax.shard_map(
        functools.partial(local, nx),
        mesh=mesh,
        in_specs=(
            P("grid", "layer", None, None),
            P("grid", "layer"),
            P("grid", None, None, None),
            P("grid", None),
        ),
        out_specs=P("grid", "layer", None, None),
        check_vma=False,
    )
```

```python
import functools

import jax
import jax.numpy as jnp
from jax import lax
from jax.experimental import pallas as pl
from jax.experimental.pallas import tpu as pltpu
from jax.sharding import PartitionSpec as P

MESH = pl.DeviceIdType.MESH
SHIFT = 64
CHUNK = 1
XCHUNKS = 1
HOP = 5
LAG = 4
PASS = 8
PLANE_ROWS = 12
GROUP = 16


def main_kernel(
    nz, nx, nl, cap, per_layer,
    tab, a_hbm, p_hbm, out_ref,
    tabv, tabs, permv, perms, a_vm, p_own, asend, arecv, metav, metar, meta_s, zbuf, xbuf, fbuf, pcbuf, pcs, ptw, wide,
    acc, tot, hsend_i, hsend_c, hrecv_i, hrecv_c,
    load_sem, as_sem, ar_sem, m_sem, zs, zr, xs, xr, fs, fr, rs, rr, gs, gr, pcss, pcr, hs, hr,
):
    half = p_own.shape[1] * CHUNK
    fine = 2 * half
    late_chunks = PLANE_ROWS // 2 // CHUNK
    early_chunks = half // CHUNK - late_chunks
    chunks = early_chunks + nx * late_chunks
    ng = nz * nx
    layer = lax.axis_index("layer")
    grid = lax.axis_index("grid")
    z, x = grid // nx, grid % nx
    d = lax.rem(z - layer + nz, nz)
    up = lax.rem(z + 1, nz) * nx + x
    down = lax.rem(z + nz - 1, nz) * nx + x
    right = z * nx + lax.rem(x + 1, nx)
    left = z * nx + lax.rem(x + nx - 1, nx)
    after, before = lax.rem(grid + 1, ng), lax.rem(grid + ng - 1, ng)
    lafter, lbefore = lax.rem(layer + 1, nl), lax.rem(layer + nl - 1, nl)

    def remote(src, dst, ssem, rsem, g, l):
        return pltpu.make_async_remote_copy(
            src_ref=src, dst_ref=dst, send_sem=ssem, recv_sem=rsem, device_id=(g, l), device_id_type=MESH
        )

    def turn(o):
        return o + o // 2 * (1 - 2 * (o % 2))

    load_p = pltpu.make_async_copy(p_hbm, p_own, load_sem.at[1])
    load_a = pltpu.make_async_copy(a_hbm, a_vm, load_sem.at[0])
    load_t = pltpu.make_async_copy(tab, tabv, load_sem.at[2])
    load_s = pltpu.make_async_copy(tab, tabs, load_sem.at[3])
    own_chunks = early_chunks + late_chunks
    first = [
        pltpu.make_async_copy(
            p_hbm.at[s],
            zbuf.at[s, pl.ds(0, own_chunks)],
            load_sem.at[4 + s],
        )
        for s in (0, 1)
    ]
    cols = pltpu.make_async_copy(tab.at[1], pcbuf.at[0], load_sem.at[6])

    @pl.when(d == 0)
    def _():
        for s in (0, 1):
            first[s].start()
        cols.start()

    load_t.start()
    load_s.start()
    load_a.start()
    load_p.start()

    barrier = pltpu.get_barrier_semaphore()
    partners = [(up, layer), (down, layer), (right, layer), (left, layer)]
    partners += [(grid, lax.rem(layer + k, nl)) for k in range(1, nl)]
    partners += [(g, l) for g in (after, before) for l in (layer, lafter, lbefore)]
    for g, l in partners:
        pl.semaphore_signal(barrier, inc=1, device_id=(g, l), device_id_type=MESH)
    pl.semaphore_wait(barrier, len(partners))

    @pl.when(d == 0)
    def _():
        for s in (0, 1):
            first[s].wait()
        cols.wait()

    def late(o):
        return pl.ds(early_chunks + o * late_chunks, late_chunks)

    def z_copy(s, c):
        return remote(zbuf.at[s, c], zbuf.at[s, c], zs.at[s], zr.at[s, c], (up, down)[s], layer)

    def x_copy(side, s, at, count):
        return remote(
            zbuf.at[s, pl.ds(at, count)], xbuf.at[side, s, pl.ds(at, count)], xs.at[side, s], xr.at[side, s],
            (right, left)[side], layer,
        )

    def x_all(side, s):
        return x_copy(side, s, 0, early_chunks)

    def f_copy(s):
        return remote(xbuf.at[s, s], fbuf.at[s], fs.at[s], fr.at[s], (right, left)[s], layer)

    def r_copy(side, s):
        return remote(
            zbuf.at[s, late(0)], zbuf.at[s, late(2 - side)], rs.at[side, s], rr.at[side, s], (right, left)[side], layer
        )

    def g_copy(s):
        return remote(zbuf.at[s, late(2 - s)], zbuf.at[s, late(3)], gs.at[s], gr.at[s], (right, left)[s], layer)

    def pc_copy(which):
        src, dst, g = ((0, 0, up), (0, 3, right), (0, 1, left), (3, 2, right))[which]
        return remote(pcbuf.at[src], pcbuf.at[dst], pcss.at[which], pcr.at[which], g, layer)

    hops = (d, lax.rem(nz - d, nz))
    near, far = jnp.minimum(*hops), jnp.maximum(*hops)
    near_turn = HOP * near
    far_turn = jnp.maximum(near_turn + early_chunks, HOP * far)
    up_first = jnp.minimum(jnp.maximum(hops[1] - hops[0] + 1, 0), 1)
    x_turn = (
        up_first * near_turn + (1 - up_first) * far_turn,
        up_first * far_turn + (1 - up_first) * near_turn,
    )
    pass_turn = jnp.maximum(far_turn + early_chunks + LAG, chunks + PASS)
    ready = jnp.maximum(early_chunks + late_chunks + HOP * far, pass_turn + 1 - late_chunks)

    def p_step(t):
        for s in (0, 1):
            hop = hops[s]
            c = t - HOP * hop

            @pl.when((c >= 0) & (c < chunks))
            def _():
                @pl.when(d != 0)
                def _():
                    z_copy(s, c).wait_recv()

                @pl.when(d == 0)
                def _():
                    @pl.when(c == early_chunks + (1 + s) * late_chunks)
                    def _():
                        r_copy(1 - s, s).wait_recv()

                    @pl.when(c == early_chunks + 3 * late_chunks)
                    def _():
                        g_copy(s).wait_recv()

                @pl.when(hop < nz - 1)
                def _():
                    z_copy(s, c).start()

                if s == 0:

                    @pl.when(c == 0)
                    def _():
                        @pl.when(d != 0)
                        def _():
                            pc_copy(0).wait_recv()

                        @pl.when(hop < nz - 1)
                        def _():
                            pc_copy(0).start()

                        pc_copy(1).start()
                        pc_copy(2).start()

                    @pl.when(c == 2)
                    def _():
                        pc_copy(1).wait_recv()
                        pc_copy(3).start()

                @pl.when((d == 0) & (c == 0))
                def _():
                    r_copy(0, s).start()
                    r_copy(1, s).start()

                @pl.when((d == 0) & (c == early_chunks))
                def _():
                    r_copy(s, s).wait_recv()
                    g_copy(s).start()

            e = t - x_turn[s]

            @pl.when((e >= 0) & (e < early_chunks) & (lax.rem(e + XCHUNKS, XCHUNKS) == XCHUNKS - 1))
            def _():
                x_copy(0, s, e - (XCHUNKS - 1), XCHUNKS).start()
                x_copy(1, s, e - (XCHUNKS - 1), XCHUNKS).start()

        @pl.when(t == pass_turn)
        def _():
            for s in (0, 1):
                x_all(s, s).wait_recv()
                f_copy(s).start()

    p_step(0)

    load_t.wait()
    size = tabv.shape[2]
    per = nx * cap
    blank = fine * SHIFT
    rows = lax.broadcasted_iota(jnp.int32, (size, size), 0)
    lanes = lax.broadcasted_iota(jnp.int32, (size, size), 1)

    def upright(v):
        return jnp.broadcast_to(v, (size, size)).T

    def count_steps(v, width, most):
        total = jnp.zeros_like(v)
        for k in range(1, most):
            total = total + jnp.where(v >= k * width, 1, 0)
        return total

    col, lane = tabv[0], lanes[0:1]
    owner_of = count_steps(col, fine, ng)
    own = jnp.where(lane < a_vm.shape[0], owner_of, SHIFT * ng)
    packed = count_steps(lane, per_layer, fine) * SHIFT + col - owner_of * fine
    same = (upright(own) == jnp.broadcast_to(own, (size, size))) & (rows < lanes)
    rank = jnp.sum(jnp.where(same, 1, 0), axis=0, keepdims=True)
    slot = upright(own * cap + rank)
    value = upright(packed - blank)
    for l in range(nl):
        hit = (slot == l * per + lanes) & (lanes < per) & (rows < a_vm.shape[0])
        permv[l] = jnp.sum(jnp.where(hit, rows, 0), axis=0, keepdims=True)
        metav[l] = blank + jnp.sum(jnp.where(hit, value, 0), axis=0, keepdims=True)
    to_smem = pltpu.make_async_copy(permv, perms, load_sem.at[7])
    to_smem.start()

    def m_copy(k):
        to = lax.rem(layer + k, nl)
        return remote(metav.at[to], metar.at[layer], m_sem.at[0], m_sem.at[1], grid, to)

    m_all = remote(metav.at[pl.ds(0, nl - 1)], metar.at[pl.ds(0, nl - 1)], m_sem.at[0], m_sem.at[1], grid, lafter)
    for k in range(1, nl):
        m_copy(k).start()
    metar[layer] = metav[layer]
    to_smem.wait()
    load_a.wait()

    def a_copy(o, k):
        to = lax.rem(layer + k, nl)
        return remote(asend.at[o * nl + k], arecv.at[o, layer], as_sem.at[o], ar_sem.at[o], grid, to)

    def a_all(o):
        part = pl.ds(0, nl - 1)
        return remote(asend.at[part], arecv.at[o, part], as_sem.at[o], ar_sem.at[o], grid, lafter)

    def a_phase(o):
        q = lax.rem(x + turn(o), nx)

        def send_a(k, unused):
            to = lax.rem(layer + k, nl)
            for c in range(cap):
                asend[o * nl + k, c] = a_vm[perms[to, 0, q * cap + c]]
            a_copy(o, k).start()
            return unused

        lax.fori_loop(1, nl, send_a, 0)
        for c in range(cap):
            arecv[o, layer, c] = a_vm[perms[layer, 0, q * cap + c]]

    a_phase(0)
    load_p.wait()
    load_s.wait()
    ptw[fine] = jnp.zeros(ptw.shape[1:], ptw.dtype)
    tot[...] = jnp.zeros_like(tot)

    def spread(ref, at, o0, o1, t0, t1, upright_blocks):
        zero = jnp.zeros_like(t0)
        for b in range(3):
            tile = jnp.where(o0 == b, t0, jnp.where(o1 == b, t1, zero))
            if upright_blocks:
                ref[at, b * 128 : (b + 1) * 128, :] = tile
            else:
                ref[at, :, b * 128 : (b + 1) * 128] = tile

    def offset(col, g):
        return lax.rem(col - g + 1 + ng, ng)

    def transpose_rows(lo):
        for r in range(4):
            i = lo * 4 + r
            o0, o1 = offset(tabs[1, 0, 2 * i], grid), offset(tabs[1, 0, 2 * i + 1], grid)
            s, c = lax.div(i, half), lax.div(lax.rem(i, half), CHUNK)
            at = (s, c, lax.rem(i, CHUNK))
            spread(ptw, i, o0, o1, p_own[at + (0,)].T, p_own[at + (1,)].T, True)

    slots = nl * cap
    widen_units, group_units = 4, slots // GROUP
    units = widen_units + group_units

    def arrive(o):
        a_all(o).wait_recv()

        @pl.when(o == 0)
        def _():
            m_all.wait_recv()
            pc_copy(2).wait_recv()
            pc_copy(3).wait_recv()
            tables = pltpu.make_async_copy(metar, meta_s, load_sem.at[2])
            tables.start()
            columns = pltpu.make_async_copy(pcbuf, pcs, load_sem.at[3])
            columns.start()
            tables.wait()
            columns.wait()

        @pl.when(o == 1)
        def _():
            x_all(1, 0).wait_recv()

        @pl.when(o == 2)
        def _():
            x_all(0, 1).wait_recv()

        @pl.when(o == 3)
        def _():
            f_copy(0).wait_recv()
            f_copy(1).wait_recv()

    def widen(o, w):
        rel = turn(o)
        owner = layer * nx + lax.rem(x + rel, nx)
        for s in (0, 1):

            def widen_row(ref, at, c, r, start):
                j = s * half + start + c * CHUNK + r
                o0, o1 = offset(pcs[rel, 0, 2 * j], owner), offset(pcs[rel, 0, 2 * j + 1], owner)
                spread(wide, j, o0, o1, ref[at + (c, r, 0)], ref[at + (c, r, 1)], False)

            for turn_of, (ref, at) in enumerate(
                ((zbuf, (s,)), (xbuf, (1, s)), (xbuf, (0, s)), (fbuf, (s,)))
            ):

                @pl.when((w == 2 * s) & (o == turn_of))
                def _():
                    def one(c, unused):
                        for r in range(CHUNK):
                            widen_row(ref, at, c, r, 0)
                        return unused

                    lax.fori_loop(0, early_chunks, one, 0)

            @pl.when(w == 2 * s + 1)
            def _():
                def one(c, unused):
                    j = s * half + early_chunks * CHUNK + c * CHUNK
                    for r in range(CHUNK):
                        o0 = offset(pcs[rel, 0, 2 * (j + r)], owner)
                        o1 = offset(pcs[rel, 0, 2 * (j + r) + 1], owner)
                        at = early_chunks + o * late_chunks + c
                        spread(wide, j + r, o0, o1, zbuf[s, at, r, 0], zbuf[s, at, r, 1], False)
                    return unused

                lax.fori_loop(0, late_chunks, one, 0)

    def some(o, u):
        q = lax.rem(x + turn(o), nx)
        lefts, prods = [], []
        for v in range(GROUP):
            n = u * GROUP + v
            src = lax.div(n, cap)
            k = n - src * cap
            m = meta_s[src, 0, q * cap + k]
            i, j = m // SHIFT, m % SHIFT
            prods.append(jnp.dot(arecv[o, src, k], wide[j], preferred_element_type=jnp.float32).astype(jnp.bfloat16))
            lefts.append(ptw[i])
        acc[...] += jnp.dot(
            jnp.concatenate(lefts, axis=1), jnp.concatenate(prods, axis=0), preferred_element_type=jnp.float32
        )

    def flush(o):
        q = lax.rem(x + turn(o), nx)
        for a in range(3):
            for b in range(3):
                tot[a, q + b] += acc[a * 128 : (a + 1) * 128, b * 128 : (b + 1) * 128]

    def unit(o, w):
        @pl.when(w == 0)
        def _():
            arrive(o)
            acc[...] = jnp.zeros_like(acc)

        @pl.when(w < widen_units)
        def _():
            widen(o, w)

        @pl.when(w >= widen_units)
        def _():
            some(o, w - widen_units)

        @pl.when(w == units - 1)
        def _():
            flush(o)

    pace = -(-units // late_chunks)

    def step(t, unused):
        p_step(t)

        @pl.when(t < nx)
        def _():
            a_phase(t)

        @pl.when(t <= fine // 4)
        def _():
            transpose_rows(t - 1)

        @pl.when(t >= ready)
        def _():
            o = lax.div(t - ready, late_chunks)
            at = t - ready - o * late_chunks

            def one(v, unused):
                w = at * pace + v

                @pl.when(w < units)
                def _():
                    unit(o, w)

                return unused

            lax.fori_loop(0, pace, one, 0)

        return unused

    lax.fori_loop(1, ready + nx * late_chunks, step, 0)

    for o in range(nx):
        a_all(o).wait_send()
    m_all.wait_send()
    for s in (0, 1):

        @pl.when(hops[s] < nz - 1)
        def _():
            remote(zbuf.at[s], zbuf.at[s], zs.at[s], zr.at[s, 0], (up, down)[s], layer).wait_send()

        x_all(0, s).wait_send()
        x_all(1, s).wait_send()
        f_copy(s).wait_send()

        @pl.when(d == 0)
        def _():
            r_copy(0, s).wait_send()
            r_copy(1, s).wait_send()
            g_copy(s).wait_send()

    @pl.when(d < nz - 1)
    def _():
        pc_copy(0).wait_send()

    for which in (1, 2, 3):
        pc_copy(which).wait_send()

    bf = jnp.bfloat16
    hsend_i[0] = tot[2, 1 : nx + 1].astype(bf)
    hsend_i[1] = tot[0, 1 : nx + 1].astype(bf)
    hsend_c[0] = tot[1, nx + 1].astype(bf)
    hsend_c[1] = tot[1, 0].astype(bf)
    hsend_c[2] = tot[2, nx + 1].astype(bf)
    hsend_c[3] = tot[2, 0].astype(bf)
    hsend_c[4] = tot[0, nx + 1].astype(bf)
    hsend_c[5] = tot[0, 0].astype(bf)
    copies = [
        remote(hsend_i.at[k], hrecv_i.at[k], hs.at[k], hr.at[k], g, layer) for k, g in enumerate((after, before))
    ]
    to = [(g, l) for g in (grid, after, before) for l in (lafter, lbefore)]
    copies += [
        remote(hsend_c.at[k], hrecv_c.at[k], hs.at[2 + k], hr.at[2 + k], g, l) for k, (g, l) in enumerate(to)
    ]
    for copy in copies:
        copy.start()
    for copy in copies:
        copy.wait_recv()
    for b in range(nx):
        total = tot[1, 1 + b]
        for k in range(2):
            total = total + hrecv_i[k, b].astype(jnp.float32)
        if b == 0:
            for k in (0, 2, 4):
                total = total + hrecv_c[k].astype(jnp.float32)
        if b == nx - 1:
            for k in (1, 3, 5):
                total = total + hrecv_c[k].astype(jnp.float32)
        out_ref[0, b] = total.astype(bf)

    for copy in copies:
        copy.wait_send()


def local(nx, a_tiles, a_cols, p_tiles, p_cols):
    fine, per_layer, size, unused = a_tiles.shape
    nl, ng = lax.axis_size("layer"), lax.axis_size("grid")
    nz = ng // nx
    slot_total = fine * per_layer
    cap = 2 * slot_total // ng
    anywhere = pl.BlockSpec(memory_space=pl.ANY)
    def lane_row(v):
        v = v.reshape(1, 1, -1)
        return jnp.pad(v, ((0, 0), (0, 0), (0, 128 - v.shape[2])))

    tab = jnp.concatenate([lane_row(a_cols), lane_row(p_cols)])
    half = fine // 2
    early_chunks = (half - PLANE_ROWS // 2) // CHUNK
    chunks = early_chunks + nx * (PLANE_ROWS // 2 // CHUNK)
    row = p_tiles.shape[1:]
    bf, f32, i32 = jnp.bfloat16, jnp.float32, jnp.int32
    dma = pltpu.SemaphoreType.DMA
    return pl.pallas_call(
        functools.partial(main_kernel, nz, nx, nl, cap, per_layer),
        out_shape=jax.ShapeDtypeStruct((1, nx, size, size), bf),
        in_specs=[anywhere, anywhere, anywhere],
        out_specs=pl.BlockSpec(memory_space=pltpu.VMEM),
        scratch_shapes=[
            pltpu.VMEM((2, 1, 128), i32),
            pltpu.SMEM((2, 1, 128), i32),
            pltpu.VMEM((nl, 1, 128), i32),
            pltpu.SMEM((nl, 1, 128), i32),
            pltpu.VMEM((slot_total, size, size), bf),
            pltpu.VMEM((2, early_chunks + PLANE_ROWS // 2 // CHUNK, CHUNK) + row, bf),
            pltpu.VMEM((ng, cap, size, size), bf),
            pltpu.VMEM((nx, nl, cap, size, size), bf),
            pltpu.VMEM((nl, 1, 128), i32),
            pltpu.VMEM((nl, 1, 128), i32),
            pltpu.SMEM((nl, 1, 128), i32),
            pltpu.VMEM((2, chunks, CHUNK) + row, bf),
            pltpu.VMEM((2, 2, early_chunks, CHUNK) + row, bf),
            pltpu.VMEM((2, early_chunks, CHUNK) + row, bf),
            pltpu.VMEM((nx, 1, 128), i32),
            pltpu.SMEM((nx, 1, 128), i32),
            pltpu.VMEM((fine + 1, 3 * size, size), bf),
            pltpu.VMEM((fine, size, 3 * size), bf),
            pltpu.VMEM((3 * size, 3 * size), f32),
            pltpu.VMEM((3, nx + 2, size, size), f32),
            pltpu.VMEM((2, nx, size, size), bf),
            pltpu.VMEM((6, size, size), bf),
            pltpu.VMEM((2, nx, size, size), bf),
            pltpu.VMEM((6, size, size), bf),
            dma((8,)),
            dma((nx,)), dma((nx,)), dma((2,)),
            dma((2,)), dma((2, chunks)),
            dma((2, 2)), dma((2, 2)),
            dma((2,)), dma((2,)),
            dma((2, 2)), dma((2, 2)), dma((2,)), dma((2,)),
            dma((4,)), dma((4,)),
            dma((8,)), dma((8,)),
        ],
        compiler_params=pltpu.CompilerParams(
            collective_id=0, has_side_effects=True, vmem_limit_bytes=58 * 1024 * 1024
        ),
    )(tab, a_tiles.reshape(slot_total, size, size), p_tiles.reshape((2, early_chunks + PLANE_ROWS // 2 // CHUNK, CHUNK) + row))


def solution(mesh):
    nx = 4
    return jax.shard_map(
        functools.partial(local, nx),
        mesh=mesh,
        in_specs=(
            P("grid", "layer", None, None),
            P("grid", "layer"),
            P("grid", None, None, None),
            P("grid", None),
        ),
        out_specs=P("grid", "layer", None, None),
        check_vma=False,
    )
```

```python
import functools

import jax
import jax.numpy as jnp
from jax import lax
from jax.experimental import pallas as pl
from jax.experimental.pallas import tpu as pltpu
from jax.sharding import PartitionSpec as P

MESH = pl.DeviceIdType.MESH
SHIFT = 64
CHUNK = 1
PARTS = 3
SPACING = 10
HOP = 4
LAG = 3
PLANE_ROWS = 12
GROUP = 24


def main_kernel(
    nz, nx, nl, cap, per_layer,
    tab, a_hbm, p_hbm, out_ref,
    tabv, tabs, permv, perms, a_vm, p_own, asend, arecv, metav, metar, meta_s, zbuf, xbuf, fbuf, pcbuf, pcs, ptw, wide,
    acc, tot, hsend_i, hsend_c, hrecv_i, hrecv_c,
    load_sem, as_sem, ar_sem, m_sem, zs, zr, xs, xr, fs, fr, rs, rr, pcss, pcr, hs, hr,
):
    half = p_own.shape[1] * CHUNK
    fine = 2 * half
    late_chunks = PLANE_ROWS // 2 // CHUNK
    early_chunks = half // CHUNK - late_chunks
    chunks = early_chunks + nx * late_chunks
    ng = nz * nx
    layer = lax.axis_index("layer")
    grid = lax.axis_index("grid")
    z, x = grid // nx, grid % nx
    d = lax.rem(z - layer + nz, nz)
    up = lax.rem(z + 1, nz) * nx + x
    down = lax.rem(z + nz - 1, nz) * nx + x
    right = z * nx + lax.rem(x + 1, nx)
    left = z * nx + lax.rem(x + nx - 1, nx)
    after, before = lax.rem(grid + 1, ng), lax.rem(grid + ng - 1, ng)
    lafter, lbefore = lax.rem(layer + 1, nl), lax.rem(layer + nl - 1, nl)

    def remote(src, dst, ssem, rsem, g, l):
        return pltpu.make_async_remote_copy(
            src_ref=src, dst_ref=dst, send_sem=ssem, recv_sem=rsem, device_id=(g, l), device_id_type=MESH
        )

    def turn(o):
        return o + o // 2 * (1 - 2 * (o % 2))

    load_p = pltpu.make_async_copy(p_hbm, p_own, load_sem.at[1])
    load_a = pltpu.make_async_copy(a_hbm, a_vm, load_sem.at[0])
    load_t = pltpu.make_async_copy(tab, tabv, load_sem.at[2])
    load_s = pltpu.make_async_copy(tab, tabs, load_sem.at[3])
    own_chunks = early_chunks + late_chunks
    first = [
        pltpu.make_async_copy(
            p_hbm.at[s],
            zbuf.at[s, pl.ds(0, own_chunks)],
            load_sem.at[4 + s],
        )
        for s in (0, 1)
    ]
    cols = pltpu.make_async_copy(tab.at[pl.ds(2, 2)], pcbuf.at[0], load_sem.at[6])

    @pl.when(d == 0)
    def _():
        for s in (0, 1):
            first[s].start()
        cols.start()

    load_t.start()
    load_s.start()
    load_a.start()
    load_p.start()

    barrier = pltpu.get_barrier_semaphore()
    partners = [(up, layer), (down, layer), (right, layer), (left, layer)]
    partners += [(grid, lax.rem(layer + k, nl)) for k in range(1, nl)]
    partners += [(g, l) for g in (after, before) for l in (layer, lafter, lbefore)]
    for g, l in partners:
        pl.semaphore_signal(barrier, inc=1, device_id=(g, l), device_id_type=MESH)

    @pl.when(d == 0)
    def _():
        for k in range(1, nx):
            for y in range(nl // 2):
                pl.semaphore_signal(
                    barrier, inc=1, device_id=(z * nx + lax.rem(x + k, nx), 2 * y + lax.rem(z, 2)), device_id_type=MESH
                )

    pl.semaphore_wait(barrier, len(partners) + (nx - 1) * (1 - lax.rem(layer + z, 2)))


    @pl.when(d == 0)
    def _():
        for s in (0, 1):
            first[s].wait()
        cols.wait()

    def late(o):
        return pl.ds(early_chunks + o * late_chunks, late_chunks)

    def z_copy(s, c):
        return remote(zbuf.at[s, c], zbuf.at[s, c], zs.at[s], zr.at[s, c], (up, down)[s], layer)

    part = early_chunks // PARTS

    def x_copy(side, s, at, count):
        return remote(
            zbuf.at[s, pl.ds(at, count)], xbuf.at[side, s, pl.ds(at, count)],
            xs.at[side, s], xr.at[side, s, lax.div(at, part)], (right, left)[side], layer,
        )

    def x_part(side, s, p):
        return x_copy(side, s, p * part, part)

    def x_sent(side, s):
        return x_copy(side, s, 0, early_chunks)

    def f_copy(s, at, count):
        return remote(
            xbuf.at[s, s, pl.ds(at, count)], fbuf.at[s, pl.ds(at, count)], fs.at[s], fr.at[s], (right, left)[s], layer
        )

    def f_all(s):
        return f_copy(s, 0, early_chunks)

    planes = nl // 2
    shares = 4 // planes
    part_chunks = late_chunks // 2
    opposite = z * nx + lax.rem(x + 2, nx)
    sends_late = lax.rem(layer, 2) == lax.rem(z, 2)

    def r_copy(k, u):
        o, g = ((2, right), (1, left), (3, opposite))[k]
        at = lax.div(layer, 2) * shares + u
        s = lax.div(at, 2)
        start = early_chunks + (at - 2 * s) * part_chunks
        return remote(
            p_own.at[s, pl.ds(start, part_chunks)], zbuf.at[s, pl.ds(start + o * late_chunks, part_chunks)],
            rs.at[k, u], rr.at[o - 1, s], g, z,
        )

    def r_all(o, s):
        return remote(zbuf.at[s, late(o)], zbuf.at[s, late(o)], rs.at[0, 0], rr.at[o - 1, s], right, layer)

    def pc_copy(which):
        src, dst, g = ((0, 0, up), (0, 3, right), (0, 1, left), (3, 2, right))[which]
        return remote(pcbuf.at[src], pcbuf.at[dst], pcss.at[which], pcr.at[which], g, layer)

    hops = (d, lax.rem(nz - d, nz))
    near, far = jnp.minimum(*hops), jnp.maximum(*hops)
    near_turn = HOP * near
    far_turn = jnp.maximum(near_turn + early_chunks, HOP * far)
    up_first = jnp.minimum(jnp.maximum(hops[1] - hops[0] + 1, 0), 1)
    x_turn = (
        up_first * near_turn + (1 - up_first) * far_turn,
        up_first * far_turn + (1 - up_first) * near_turn,
    )
    pass_turn = far_turn + early_chunks // PARTS + LAG
    first_turn = early_chunks + late_chunks + HOP * far
    rest_turn = jnp.maximum(first_turn + late_chunks, pass_turn + (PARTS - 1) * SPACING + 1)

    def p_step(t):
        for s in (0, 1):
            hop = hops[s]
            c = t - HOP * hop

            @pl.when((c >= 0) & (c < chunks))
            def _():
                @pl.when(d != 0)
                def _():
                    z_copy(s, c).wait_recv()

                @pl.when(d == 0)
                def _():
                    for o in range(1, nx):

                        @pl.when(c == early_chunks + o * late_chunks)
                        def _():
                            r_all(o, s).wait_recv()

                @pl.when(hop < nz - 1)
                def _():
                    z_copy(s, c).start()

                if s == 0:

                    @pl.when(c == 0)
                    def _():
                        @pl.when(d != 0)
                        def _():
                            pc_copy(0).wait_recv()

                        @pl.when(hop < nz - 1)
                        def _():
                            pc_copy(0).start()

                        pc_copy(1).start()
                        pc_copy(2).start()

                    @pl.when(c == 2)
                    def _():
                        pc_copy(1).wait_recv()
                        pc_copy(3).start()

            e = t - x_turn[s]

            @pl.when((e >= 0) & (e < early_chunks))
            def _():
                x_copy(0, s, e, 1).start()
                x_copy(1, s, e, 1).start()

        for p in range(PARTS):

            @pl.when(t == pass_turn + p * SPACING)
            def _():
                for s in (0, 1):
                    x_part(s, s, p).wait_recv()
                    f_copy(s, p * part, part).start()

    p_step(0)

    load_t.wait()
    size = tabv.shape[2]
    per = nx * cap
    blank = fine * SHIFT
    rows = lax.broadcasted_iota(jnp.int32, (size, size), 0)
    lanes = lax.broadcasted_iota(jnp.int32, (size, size), 1)

    def upright(v):
        return jnp.broadcast_to(v, (size, size)).T

    def count_steps(v, width, most):
        total = jnp.zeros_like(v)
        for k in range(1, most):
            total = total + jnp.where(v >= k * width, 1, 0)
        return total

    lane = lanes[0:1]
    second = jnp.where(lane >= 64, 1, 0)
    col = jnp.where(lane >= 64, pltpu.roll(tabv[1], 64, 1), tabv[0])
    row = lane - 64 * second
    tile = 2 * rows - 127 * jnp.where(rows >= 64, 1, 0)
    owner_of = count_steps(col, fine, ng)
    own = jnp.where(row < fine, owner_of, SHIFT * ng)
    packed = row * SHIFT + col - owner_of * fine
    same = (upright(own) == jnp.broadcast_to(own, (size, size))) & (rows < lanes)
    rank = jnp.sum(jnp.where(same, 1, 0), axis=0, keepdims=True)
    slot = upright(own * cap + rank)
    value = upright(packed - blank)
    for l in range(nl):
        hit = (slot == l * per + lanes) & (lanes < per)
        permv[l] = jnp.sum(jnp.where(hit, tile, 0), axis=0, keepdims=True)
        metav[l] = blank + jnp.sum(jnp.where(hit, value, 0), axis=0, keepdims=True)
    to_smem = pltpu.make_async_copy(permv, perms, load_sem.at[7])
    to_smem.start()

    def m_copy(k):
        to = lax.rem(layer + k, nl)
        return remote(metav.at[to], metar.at[layer], m_sem.at[0], m_sem.at[1], grid, to)

    m_all = remote(metav.at[pl.ds(0, nl - 1)], metar.at[pl.ds(0, nl - 1)], m_sem.at[0], m_sem.at[1], grid, lafter)
    for k in range(1, nl):
        m_copy(k).start()
    metar[layer] = metav[layer]
    to_smem.wait()
    load_a.wait()

    def a_copy(o, k):
        to = lax.rem(layer + k, nl)
        return remote(asend.at[o * nl + k], arecv.at[o, layer], as_sem.at[o], ar_sem.at[o], grid, to)

    def a_all(o):
        part = pl.ds(0, nl - 1)
        return remote(asend.at[part], arecv.at[o, part], as_sem.at[o], ar_sem.at[o], grid, lafter)

    def a_phase(o):
        q = lax.rem(x + turn(o), nx)

        def send_a(k, unused):
            to = lax.rem(layer + k, nl)
            for c in range(cap):
                asend[o * nl + k, c] = a_vm[perms[to, 0, q * cap + c]]
            a_copy(o, k).start()
            return unused

        lax.fori_loop(1, nl, send_a, 0)
        for c in range(cap):
            arecv[o, layer, c] = a_vm[perms[layer, 0, q * cap + c]]

    load_p.wait()

    @pl.when(sends_late)
    def _():
        for k in range(3):
            for u in range(shares):
                r_copy(k, u).start()

    a_phase(0)
    load_s.wait()
    ptw[fine] = jnp.zeros(ptw.shape[1:], ptw.dtype)
    tot[...] = jnp.zeros_like(tot)

    def spread(ref, at, o0, o1, t0, t1, upright_blocks):
        zero = jnp.zeros_like(t0)
        for b in range(3):
            tile = jnp.where(o0 == b, t0, jnp.where(o1 == b, t1, zero))
            if upright_blocks:
                ref[at, b * 128 : (b + 1) * 128, :] = tile
            else:
                ref[at, :, b * 128 : (b + 1) * 128] = tile

    def offset(col, g):
        return lax.rem(col - g + 1 + ng, ng)

    def transpose_rows(lo):
        for r in range(4):
            i = lo * 4 + r
            o0, o1 = offset(tabs[2, 0, i], grid), offset(tabs[3, 0, i], grid)
            s, c = lax.div(i, half), lax.div(lax.rem(i, half), CHUNK)
            at = (s, c, lax.rem(i, CHUNK))
            spread(ptw, i, o0, o1, p_own[at + (0,)].T, p_own[at + (1,)].T, True)

    slots = nl * cap
    widen_units, group_units = 4, slots // GROUP
    units = widen_units + group_units

    def arrive(o):
        a_all(o).wait_recv()

        @pl.when(o == 0)
        def _():
            m_all.wait_recv()
            pc_copy(2).wait_recv()
            pc_copy(3).wait_recv()
            tables = pltpu.make_async_copy(metar, meta_s, load_sem.at[2])
            tables.start()
            columns = pltpu.make_async_copy(pcbuf, pcs, load_sem.at[3])
            columns.start()
            tables.wait()
            columns.wait()

        @pl.when(o == 1)
        def _():
            for p in range(PARTS):
                x_part(1, 0, p).wait_recv()

        @pl.when(o == 2)
        def _():
            for p in range(PARTS):
                x_part(0, 1, p).wait_recv()

        @pl.when(o == 3)
        def _():
            f_all(0).wait_recv()
            f_all(1).wait_recv()

    def widen(o, w):
        rel = turn(o)
        owner = layer * nx + lax.rem(x + rel, nx)
        for s in (0, 1):

            def widen_row(ref, at, c, r, start):
                j = s * half + start + c * CHUNK + r
                o0, o1 = offset(pcs[rel, 0, 0, j], owner), offset(pcs[rel, 1, 0, j], owner)
                spread(wide, j, o0, o1, ref[at + (c, r, 0)], ref[at + (c, r, 1)], False)

            for turn_of, (ref, at) in enumerate(
                ((zbuf, (s,)), (xbuf, (1, s)), (xbuf, (0, s)), (fbuf, (s,)))
            ):

                @pl.when((w == 2 * s) & (o == turn_of))
                def _():
                    def one(c, unused):
                        for r in range(CHUNK):
                            widen_row(ref, at, c, r, 0)
                        return unused

                    lax.fori_loop(0, early_chunks, one, 0)

            @pl.when(w == 2 * s + 1)
            def _():
                def one(c, unused):
                    j = s * half + early_chunks * CHUNK + c * CHUNK
                    for r in range(CHUNK):
                        o0 = offset(pcs[rel, 0, 0, j + r], owner)
                        o1 = offset(pcs[rel, 1, 0, j + r], owner)
                        at = early_chunks + o * late_chunks + c
                        spread(wide, j + r, o0, o1, zbuf[s, at, r, 0], zbuf[s, at, r, 1], False)
                    return unused

                lax.fori_loop(0, late_chunks, one, 0)

    def some(o, u):
        q = lax.rem(x + turn(o), nx)
        lefts, prods = [], []
        for v in range(GROUP):
            n = u * GROUP + v
            src = lax.div(n, cap)
            k = n - src * cap
            m = meta_s[src, 0, q * cap + k]
            i, j = m // SHIFT, m % SHIFT
            prods.append(jnp.dot(arecv[o, src, k], wide[j], preferred_element_type=jnp.float32).astype(jnp.bfloat16))
            lefts.append(ptw[i])
        acc[...] += jnp.dot(
            jnp.concatenate(lefts, axis=1), jnp.concatenate(prods, axis=0), preferred_element_type=jnp.float32
        )

    def flush(o):
        q = lax.rem(x + turn(o), nx)
        for a in range(3):
            for b in range(3):
                tot[a, q + b] += acc[a * 128 : (a + 1) * 128, b * 128 : (b + 1) * 128]

    def unit(o, w):
        @pl.when(w == 0)
        def _():
            arrive(o)
            acc[...] = jnp.zeros_like(acc)

        @pl.when(w < widen_units)
        def _():
            widen(o, w)

        @pl.when(w >= widen_units)
        def _():
            some(o, w - widen_units)

        @pl.when(w == units - 1)
        def _():
            flush(o)

    pace = -(-units // late_chunks)

    def step(t, unused):
        p_step(t)

        @pl.when(t < nx)
        def _():
            a_phase(t)

        @pl.when(t <= fine // 4)
        def _():
            transpose_rows(t - 1)

        @pl.when((t >= first_turn) & ((t < first_turn + late_chunks) | (t >= rest_turn)))
        def _():
            rest = jnp.minimum(jnp.maximum(t - rest_turn + 1, 0), 1)
            since = t - first_turn - rest * (rest_turn - late_chunks - first_turn)
            o = lax.div(since, late_chunks)
            at = since - o * late_chunks

            def one(v, unused):
                w = at * pace + v

                @pl.when(w < units)
                def _():
                    unit(o, w)

                return unused

            lax.fori_loop(0, pace, one, 0)

        return unused

    lax.fori_loop(1, rest_turn + (nx - 1) * late_chunks, step, 0)

    bf = jnp.bfloat16
    hsend_i[0] = tot[2, 1 : nx + 1].astype(bf)
    hsend_i[1] = tot[0, 1 : nx + 1].astype(bf)
    hsend_c[0] = tot[1, nx + 1].astype(bf)
    hsend_c[1] = tot[1, 0].astype(bf)
    hsend_c[2] = tot[2, nx + 1].astype(bf)
    hsend_c[3] = tot[2, 0].astype(bf)
    hsend_c[4] = tot[0, nx + 1].astype(bf)
    hsend_c[5] = tot[0, 0].astype(bf)
    copies = [
        remote(hsend_i.at[k], hrecv_i.at[k], hs.at[k], hr.at[k], g, layer) for k, g in enumerate((after, before))
    ]
    to = [(g, l) for g in (grid, after, before) for l in (lafter, lbefore)]
    copies += [
        remote(hsend_c.at[k], hrecv_c.at[k], hs.at[2 + k], hr.at[2 + k], g, l) for k, (g, l) in enumerate(to)
    ]
    for copy in copies:
        copy.start()
    for o in range(nx):
        a_all(o).wait_send()
    m_all.wait_send()
    for s in (0, 1):

        @pl.when(hops[s] < nz - 1)
        def _():
            remote(zbuf.at[s], zbuf.at[s], zs.at[s], zr.at[s, 0], (up, down)[s], layer).wait_send()

        x_sent(0, s).wait_send()
        x_sent(1, s).wait_send()
        f_all(s).wait_send()

    @pl.when(sends_late)
    def _():
        for k in range(3):
            for u in range(shares):
                r_copy(k, u).wait_send()

    @pl.when(d < nz - 1)
    def _():
        pc_copy(0).wait_send()

    for which in (1, 2, 3):
        pc_copy(which).wait_send()

    for copy in copies:
        copy.wait_recv()
    for b in range(nx):
        total = tot[1, 1 + b]
        for k in range(2):
            total = total + hrecv_i[k, b].astype(jnp.float32)
        if b == 0:
            for k in (0, 2, 4):
                total = total + hrecv_c[k].astype(jnp.float32)
        if b == nx - 1:
            for k in (1, 3, 5):
                total = total + hrecv_c[k].astype(jnp.float32)
        out_ref[0, b] = total.astype(bf)

    for copy in copies:
        copy.wait_send()


def local(nx, a_tiles, a_cols, p_tiles, p_cols):
    fine, per_layer, size, unused = a_tiles.shape
    nl, ng = lax.axis_size("layer"), lax.axis_size("grid")
    nz = ng // nx
    slot_total = fine * per_layer
    cap = 2 * slot_total // ng
    anywhere = pl.BlockSpec(memory_space=pl.ANY)
    tab = jnp.concatenate([a_cols.T, p_cols.T])
    tab = jnp.pad(tab, ((0, 0), (0, 128 - fine))).reshape(2 * per_layer, 1, 128)
    half = fine // 2
    early_chunks = (half - PLANE_ROWS // 2) // CHUNK
    chunks = early_chunks + nx * (PLANE_ROWS // 2 // CHUNK)
    row = p_tiles.shape[1:]
    bf, f32, i32 = jnp.bfloat16, jnp.float32, jnp.int32
    dma = pltpu.SemaphoreType.DMA
    return pl.pallas_call(
        functools.partial(main_kernel, nz, nx, nl, cap, per_layer),
        out_shape=jax.ShapeDtypeStruct((1, nx, size, size), bf),
        in_specs=[anywhere, anywhere, anywhere],
        out_specs=pl.BlockSpec(memory_space=pltpu.VMEM),
        scratch_shapes=[
            pltpu.VMEM((4, 1, 128), i32),
            pltpu.SMEM((4, 1, 128), i32),
            pltpu.VMEM((nl, 1, 128), i32),
            pltpu.SMEM((nl, 1, 128), i32),
            pltpu.VMEM((slot_total, size, size), bf),
            pltpu.VMEM((2, early_chunks + PLANE_ROWS // 2 // CHUNK, CHUNK) + row, bf),
            pltpu.VMEM((ng, cap, size, size), bf),
            pltpu.VMEM((nx, nl, cap, size, size), bf),
            pltpu.VMEM((nl, 1, 128), i32),
            pltpu.VMEM((nl, 1, 128), i32),
            pltpu.SMEM((nl, 1, 128), i32),
            pltpu.VMEM((2, chunks, CHUNK) + row, bf),
            pltpu.VMEM((2, 2, early_chunks, CHUNK) + row, bf),
            pltpu.VMEM((2, early_chunks, CHUNK) + row, bf),
            pltpu.VMEM((nx, 2, 1, 128), i32),
            pltpu.SMEM((nx, 2, 1, 128), i32),
            pltpu.VMEM((fine + 1, 3 * size, size), bf),
            pltpu.VMEM((fine, size, 3 * size), bf),
            pltpu.VMEM((3 * size, 3 * size), f32),
            pltpu.VMEM((3, nx + 2, size, size), f32),
            pltpu.VMEM((2, nx, size, size), bf),
            pltpu.VMEM((6, size, size), bf),
            pltpu.VMEM((2, nx, size, size), bf),
            pltpu.VMEM((6, size, size), bf),
            dma((8,)),
            dma((nx,)), dma((nx,)), dma((2,)),
            dma((2,)), dma((2, chunks)),
            dma((2, 2)), dma((2, 2, PARTS)),
            dma((2,)), dma((2,)),
            dma((3, 4)), dma((3, 2)),
            dma((4,)), dma((4,)),
            dma((8,)), dma((8,)),
        ],
        compiler_params=pltpu.CompilerParams(
            collective_id=0, has_side_effects=True, vmem_limit_bytes=58 * 1024 * 1024
        ),
    )(tab, a_tiles.reshape(slot_total, size, size), p_tiles.reshape((2, early_chunks + PLANE_ROWS // 2 // CHUNK, CHUNK) + row))


def solution(mesh):
    nx = 4
    return jax.shard_map(
        functools.partial(local, nx),
        mesh=mesh,
        in_specs=(
            P("grid", "layer", None, None),
            P("grid", "layer"),
            P("grid", None, None, None),
            P("grid", None),
        ),
        out_specs=P("grid", "layer", None, None),
        check_vma=False,
    )
```

```python
import functools

import jax
import jax.numpy as jnp
from jax import lax
from jax.experimental import pallas as pl
from jax.experimental.pallas import tpu as pltpu
from jax.sharding import PartitionSpec as P

MESH = pl.DeviceIdType.MESH
SHIFT = 64
CHUNK = 1
PARTS = 6
SPACING = 5
HOP = 4
LAG = 3
PLANE_ROWS = 12
GROUP = 24


def main_kernel(
    nz, nx, nl, cap, per_layer,
    tab, a_hbm, p_hbm, out_ref,
    tabv, tabs, permv, perms, a_vm, p_own, asend, arecv, metav, metar, meta_s, zbuf, xbuf, fbuf, pcbuf, pcs, ptw, wide,
    acc, tot, hsend_i, hsend_c, hrecv_i, hrecv_c,
    load_sem, as_sem, ar_sem, m_sem, zs, zr, xs, xr, fs, fr, rs, rr, pcss, pcr, hs, hr,
):
    half = p_own.shape[1] * CHUNK
    fine = 2 * half
    late_chunks = PLANE_ROWS // 2 // CHUNK
    early_chunks = half // CHUNK - late_chunks
    chunks = early_chunks + nx * late_chunks
    ng = nz * nx
    layer = lax.axis_index("layer")
    grid = lax.axis_index("grid")
    z, x = grid // nx, grid % nx
    d = lax.rem(z - layer + nz, nz)
    up = lax.rem(z + 1, nz) * nx + x
    down = lax.rem(z + nz - 1, nz) * nx + x
    right = z * nx + lax.rem(x + 1, nx)
    left = z * nx + lax.rem(x + nx - 1, nx)
    after, before = lax.rem(grid + 1, ng), lax.rem(grid + ng - 1, ng)
    lafter, lbefore = lax.rem(layer + 1, nl), lax.rem(layer + nl - 1, nl)

    def remote(src, dst, ssem, rsem, g, l):
        return pltpu.make_async_remote_copy(
            src_ref=src, dst_ref=dst, send_sem=ssem, recv_sem=rsem, device_id=(g, l), device_id_type=MESH
        )

    def turn(o):
        return o + o // 2 * (1 - 2 * (o % 2))

    load_p = pltpu.make_async_copy(p_hbm, p_own, load_sem.at[1])
    load_a = pltpu.make_async_copy(a_hbm, a_vm, load_sem.at[0])
    load_t = pltpu.make_async_copy(tab, tabv, load_sem.at[2])
    load_s = pltpu.make_async_copy(tab, tabs, load_sem.at[3])
    own_chunks = early_chunks + late_chunks
    first = [
        pltpu.make_async_copy(
            p_hbm.at[s],
            zbuf.at[s, pl.ds(0, own_chunks)],
            load_sem.at[4 + s],
        )
        for s in (0, 1)
    ]
    cols = pltpu.make_async_copy(tab.at[pl.ds(2, 2)], pcbuf.at[0], load_sem.at[6])

    @pl.when(d == 0)
    def _():
        for s in (0, 1):
            first[s].start()
        cols.start()

    load_t.start()
    load_s.start()
    load_a.start()
    load_p.start()

    barrier = pltpu.get_barrier_semaphore()
    partners = [(up, layer), (down, layer), (right, layer), (left, layer)]
    partners += [(grid, lax.rem(layer + k, nl)) for k in range(1, nl)]
    partners += [(g, l) for g in (after, before) for l in (layer, lafter, lbefore)]
    for g, l in partners:
        pl.semaphore_signal(barrier, inc=1, device_id=(g, l), device_id_type=MESH)

    @pl.when(d == 0)
    def _():
        for k in range(1, nx):
            for y in range(nl // 2):
                pl.semaphore_signal(
                    barrier, inc=1, device_id=(z * nx + lax.rem(x + k, nx), 2 * y + lax.rem(z, 2)), device_id_type=MESH
                )

    pl.semaphore_wait(barrier, len(partners) + (nx - 1) * (1 - lax.rem(layer + z, 2)))


    @pl.when(d == 0)
    def _():
        for s in (0, 1):
            first[s].wait()
        cols.wait()

    def late(o):
        return pl.ds(early_chunks + o * late_chunks, late_chunks)

    def z_copy(s, c):
        return remote(zbuf.at[s, c], zbuf.at[s, c], zs.at[s], zr.at[s, c], (up, down)[s], layer)

    part = early_chunks // PARTS

    def x_copy(side, s, at, count):
        return remote(
            zbuf.at[s, pl.ds(at, count)], xbuf.at[side, s, pl.ds(at, count)],
            xs.at[side, s], xr.at[side, s, lax.div(at, part)], (right, left)[side], layer,
        )

    def x_part(side, s, p):
        return x_copy(side, s, p * part, part)

    def x_sent(side, s):
        return x_copy(side, s, 0, early_chunks)

    def f_copy(s, at, count):
        return remote(
            xbuf.at[s, s, pl.ds(at, count)], fbuf.at[s, pl.ds(at, count)], fs.at[s], fr.at[s], (right, left)[s], layer
        )

    def f_all(s):
        return f_copy(s, 0, early_chunks)

    planes = nl // 2
    shares = 4 // planes
    part_chunks = late_chunks // 2
    opposite = z * nx + lax.rem(x + 2, nx)
    sends_late = lax.rem(layer, 2) == lax.rem(z, 2)

    def r_copy(k, u):
        o, g = ((2, right), (1, left), (3, opposite))[k]
        at = lax.div(layer, 2) * shares + u
        s = lax.div(at, 2)
        start = early_chunks + (at - 2 * s) * part_chunks
        return remote(
            p_own.at[s, pl.ds(start, part_chunks)], zbuf.at[s, pl.ds(start + o * late_chunks, part_chunks)],
            rs.at[k, u], rr.at[o - 1, s], g, z,
        )

    def r_all(o, s):
        return remote(zbuf.at[s, late(o)], zbuf.at[s, late(o)], rs.at[0, 0], rr.at[o - 1, s], right, layer)

    def pc_copy(which):
        src, dst, g = ((0, 0, up), (0, 3, right), (0, 1, left), (3, 2, right))[which]
        return remote(pcbuf.at[src], pcbuf.at[dst], pcss.at[which], pcr.at[which], g, layer)

    hops = (d, lax.rem(nz - d, nz))
    near, far = jnp.minimum(*hops), jnp.maximum(*hops)
    near_turn = HOP * near
    far_turn = jnp.maximum(near_turn + early_chunks, HOP * far)
    up_first = jnp.minimum(jnp.maximum(hops[1] - hops[0] + 1, 0), 1)
    x_turn = (
        up_first * near_turn + (1 - up_first) * far_turn,
        up_first * far_turn + (1 - up_first) * near_turn,
    )
    pass_turn = far_turn + early_chunks // PARTS + LAG
    first_turn = early_chunks + late_chunks + HOP * far
    rest_turn = jnp.maximum(first_turn + late_chunks, pass_turn + (PARTS - 1) * SPACING + 1)

    def p_step(t):
        for s in (0, 1):
            hop = hops[s]
            c = t - HOP * hop

            @pl.when((c >= 0) & (c < chunks))
            def _():
                @pl.when(d != 0)
                def _():
                    z_copy(s, c).wait_recv()

                @pl.when(d == 0)
                def _():
                    for o in range(1, nx):

                        @pl.when(c == early_chunks + o * late_chunks)
                        def _():
                            r_all(o, s).wait_recv()

                @pl.when(hop < nz - 1)
                def _():
                    z_copy(s, c).start()

                if s == 0:

                    @pl.when(c == 0)
                    def _():
                        @pl.when(d != 0)
                        def _():
                            pc_copy(0).wait_recv()

                        @pl.when(hop < nz - 1)
                        def _():
                            pc_copy(0).start()

                        pc_copy(1).start()
                        pc_copy(2).start()

                    @pl.when(c == 2)
                    def _():
                        pc_copy(1).wait_recv()
                        pc_copy(3).start()

            e = t - x_turn[s]

            @pl.when((e >= 0) & (e < early_chunks))
            def _():
                x_copy(0, s, e, 1).start()
                x_copy(1, s, e, 1).start()

        for p in range(PARTS):

            @pl.when(t == pass_turn + p * SPACING)
            def _():
                for s in (0, 1):
                    x_part(s, s, p).wait_recv()
                    f_copy(s, p * part, part).start()

    p_step(0)

    load_t.wait()
    size = tabv.shape[2]
    per = nx * cap
    blank = fine * SHIFT
    rows = lax.broadcasted_iota(jnp.int32, (size, size), 0)
    lanes = lax.broadcasted_iota(jnp.int32, (size, size), 1)

    def upright(v):
        return jnp.broadcast_to(v, (size, size)).T

    def count_steps(v, width, most):
        total = jnp.zeros_like(v)
        for k in range(1, most):
            total = total + jnp.where(v >= k * width, 1, 0)
        return total

    lane = lanes[0:1]
    second = jnp.where(lane >= 64, 1, 0)
    col = jnp.where(lane >= 64, pltpu.roll(tabv[1], 64, 1), tabv[0])
    row = lane - 64 * second
    tile = 2 * rows - 127 * jnp.where(rows >= 64, 1, 0)
    owner_of = count_steps(col, fine, ng)
    own = jnp.where(row < fine, owner_of, SHIFT * ng)
    packed = row * SHIFT + col - owner_of * fine
    same = (upright(own) == jnp.broadcast_to(own, (size, size))) & (rows < lanes)
    rank = jnp.sum(jnp.where(same, 1, 0), axis=0, keepdims=True)
    slot = upright(own * cap + rank)
    value = upright(packed - blank)
    for l in range(nl):
        hit = (slot == l * per + lanes) & (lanes < per)
        permv[l] = jnp.sum(jnp.where(hit, tile, 0), axis=0, keepdims=True)
        metav[l] = blank + jnp.sum(jnp.where(hit, value, 0), axis=0, keepdims=True)
    to_smem = pltpu.make_async_copy(permv, perms, load_sem.at[7])
    to_smem.start()

    def m_copy(k):
        to = lax.rem(layer + k, nl)
        return remote(metav.at[to], metar.at[layer], m_sem.at[0], m_sem.at[1], grid, to)

    m_all = remote(metav.at[pl.ds(0, nl - 1)], metar.at[pl.ds(0, nl - 1)], m_sem.at[0], m_sem.at[1], grid, lafter)
    for k in range(1, nl):
        m_copy(k).start()
    metar[layer] = metav[layer]
    to_smem.wait()
    load_a.wait()

    def a_copy(o, k):
        to = lax.rem(layer + k, nl)
        return remote(asend.at[o * nl + k], arecv.at[o, layer], as_sem.at[o], ar_sem.at[o], grid, to)

    def a_all(o):
        part = pl.ds(0, nl - 1)
        return remote(asend.at[part], arecv.at[o, part], as_sem.at[o], ar_sem.at[o], grid, lafter)

    def a_phase(o):
        q = lax.rem(x + turn(o), nx)

        def send_a(k, unused):
            to = lax.rem(layer + k, nl)
            for c in range(cap):
                asend[o * nl + k, c] = a_vm[perms[to, 0, q * cap + c]]
            a_copy(o, k).start()
            return unused

        lax.fori_loop(1, nl, send_a, 0)
        for c in range(cap):
            arecv[o, layer, c] = a_vm[perms[layer, 0, q * cap + c]]

    load_p.wait()

    @pl.when(sends_late)
    def _():
        for k in range(3):
            for u in range(shares):
                r_copy(k, u).start()

    a_phase(0)
    load_s.wait()
    ptw[fine] = jnp.zeros(ptw.shape[1:], ptw.dtype)
    tot[...] = jnp.zeros_like(tot)

    def spread(ref, at, o0, o1, t0, t1, upright_blocks):
        zero = jnp.zeros_like(t0)
        for b in range(3):
            tile = jnp.where(o0 == b, t0, jnp.where(o1 == b, t1, zero))
            if upright_blocks:
                ref[at, b * 128 : (b + 1) * 128, :] = tile
            else:
                ref[at, :, b * 128 : (b + 1) * 128] = tile

    def offset(col, g):
        return lax.rem(col - g + 1 + ng, ng)

    def transpose_rows(lo):
        for r in range(4):
            i = lo * 4 + r
            o0, o1 = offset(tabs[2, 0, i], grid), offset(tabs[3, 0, i], grid)
            s, c = lax.div(i, half), lax.div(lax.rem(i, half), CHUNK)
            at = (s, c, lax.rem(i, CHUNK))
            spread(ptw, i, o0, o1, p_own[at + (0,)].T, p_own[at + (1,)].T, True)

    slots = nl * cap
    widen_units, group_units = 4, slots // GROUP
    units = widen_units + group_units

    def arrive(o):
        a_all(o).wait_recv()

        @pl.when(o == 0)
        def _():
            m_all.wait_recv()
            pc_copy(2).wait_recv()
            pc_copy(3).wait_recv()
            tables = pltpu.make_async_copy(metar, meta_s, load_sem.at[2])
            tables.start()
            columns = pltpu.make_async_copy(pcbuf, pcs, load_sem.at[3])
            columns.start()
            tables.wait()
            columns.wait()

        @pl.when(o == 1)
        def _():
            for p in range(PARTS):
                x_part(1, 0, p).wait_recv()

        @pl.when(o == 2)
        def _():
            for p in range(PARTS):
                x_part(0, 1, p).wait_recv()

        @pl.when(o == 3)
        def _():
            f_all(0).wait_recv()
            f_all(1).wait_recv()

    def widen(o, w):
        rel = turn(o)
        owner = layer * nx + lax.rem(x + rel, nx)
        for s in (0, 1):

            def widen_row(ref, at, c, r, start):
                j = s * half + start + c * CHUNK + r
                o0, o1 = offset(pcs[rel, 0, 0, j], owner), offset(pcs[rel, 1, 0, j], owner)
                spread(wide, j, o0, o1, ref[at + (c, r, 0)], ref[at + (c, r, 1)], False)

            for turn_of, (ref, at) in enumerate(
                ((zbuf, (s,)), (xbuf, (1, s)), (xbuf, (0, s)), (fbuf, (s,)))
            ):

                @pl.when((w == 2 * s) & (o == turn_of))
                def _():
                    def one(c, unused):
                        for r in range(CHUNK):
                            widen_row(ref, at, c, r, 0)
                        return unused

                    lax.fori_loop(0, early_chunks, one, 0)

            @pl.when(w == 2 * s + 1)
            def _():
                def one(c, unused):
                    j = s * half + early_chunks * CHUNK + c * CHUNK
                    for r in range(CHUNK):
                        o0 = offset(pcs[rel, 0, 0, j + r], owner)
                        o1 = offset(pcs[rel, 1, 0, j + r], owner)
                        at = early_chunks + o * late_chunks + c
                        spread(wide, j + r, o0, o1, zbuf[s, at, r, 0], zbuf[s, at, r, 1], False)
                    return unused

                lax.fori_loop(0, late_chunks, one, 0)

    def some(o, u):
        q = lax.rem(x + turn(o), nx)
        lefts, prods = [], []
        for v in range(GROUP):
            n = u * GROUP + v
            src = lax.div(n, cap)
            k = n - src * cap
            m = meta_s[src, 0, q * cap + k]
            i, j = m // SHIFT, m % SHIFT
            prods.append(jnp.dot(arecv[o, src, k], wide[j], preferred_element_type=jnp.float32).astype(jnp.bfloat16))
            lefts.append(ptw[i])
        acc[...] += jnp.dot(
            jnp.concatenate(lefts, axis=1), jnp.concatenate(prods, axis=0), preferred_element_type=jnp.float32
        )

    def flush(o):
        q = lax.rem(x + turn(o), nx)
        for a in range(3):
            for b in range(3):
                tot[a, q + b] += acc[a * 128 : (a + 1) * 128, b * 128 : (b + 1) * 128]

    def unit(o, w):
        @pl.when(w == 0)
        def _():
            arrive(o)
            acc[...] = jnp.zeros_like(acc)

        @pl.when(w < widen_units)
        def _():
            widen(o, w)

        @pl.when(w >= widen_units)
        def _():
            some(o, w - widen_units)

        @pl.when(w == units - 1)
        def _():
            flush(o)

    pace = -(-units // late_chunks)

    def step(t, unused):
        p_step(t)

        @pl.when(t < nx)
        def _():
            a_phase(t)

        @pl.when(t <= fine // 4)
        def _():
            transpose_rows(t - 1)

        @pl.when((t >= first_turn) & ((t < first_turn + late_chunks) | (t >= rest_turn)))
        def _():
            rest = jnp.minimum(jnp.maximum(t - rest_turn + 1, 0), 1)
            since = t - first_turn - rest * (rest_turn - late_chunks - first_turn)
            o = lax.div(since, late_chunks)
            at = since - o * late_chunks

            def one(v, unused):
                w = at * pace + v

                @pl.when(w < units)
                def _():
                    unit(o, w)

                return unused

            lax.fori_loop(0, pace, one, 0)

        return unused

    lax.fori_loop(1, rest_turn + (nx - 1) * late_chunks, step, 0)

    bf = jnp.bfloat16
    hsend_i[0] = tot[2, 1 : nx + 1].astype(bf)
    hsend_i[1] = tot[0, 1 : nx + 1].astype(bf)
    hsend_c[0] = tot[1, nx + 1].astype(bf)
    hsend_c[1] = tot[1, 0].astype(bf)
    hsend_c[2] = tot[2, nx + 1].astype(bf)
    hsend_c[3] = tot[2, 0].astype(bf)
    hsend_c[4] = tot[0, nx + 1].astype(bf)
    hsend_c[5] = tot[0, 0].astype(bf)
    copies = [
        remote(hsend_i.at[k], hrecv_i.at[k], hs.at[k], hr.at[k], g, layer) for k, g in enumerate((after, before))
    ]
    to = [(g, l) for g in (grid, after, before) for l in (lafter, lbefore)]
    copies += [
        remote(hsend_c.at[k], hrecv_c.at[k], hs.at[2 + k], hr.at[2 + k], g, l) for k, (g, l) in enumerate(to)
    ]
    for copy in copies:
        copy.start()
    for o in range(nx):
        a_all(o).wait_send()
    m_all.wait_send()
    for s in (0, 1):

        @pl.when(hops[s] < nz - 1)
        def _():
            remote(zbuf.at[s], zbuf.at[s], zs.at[s], zr.at[s, 0], (up, down)[s], layer).wait_send()

        x_sent(0, s).wait_send()
        x_sent(1, s).wait_send()
        f_all(s).wait_send()

    @pl.when(sends_late)
    def _():
        for k in range(3):
            for u in range(shares):
                r_copy(k, u).wait_send()

    @pl.when(d < nz - 1)
    def _():
        pc_copy(0).wait_send()

    for which in (1, 2, 3):
        pc_copy(which).wait_send()

    for copy in copies:
        copy.wait_recv()
    for b in range(nx):
        total = tot[1, 1 + b]
        for k in range(2):
            total = total + hrecv_i[k, b].astype(jnp.float32)
        if b == 0:
            for k in (0, 2, 4):
                total = total + hrecv_c[k].astype(jnp.float32)
        if b == nx - 1:
            for k in (1, 3, 5):
                total = total + hrecv_c[k].astype(jnp.float32)
        out_ref[0, b] = total.astype(bf)

    for copy in copies:
        copy.wait_send()


def local(nx, a_tiles, a_cols, p_tiles, p_cols):
    fine, per_layer, size, unused = a_tiles.shape
    nl, ng = lax.axis_size("layer"), lax.axis_size("grid")
    nz = ng // nx
    slot_total = fine * per_layer
    cap = 2 * slot_total // ng
    anywhere = pl.BlockSpec(memory_space=pl.ANY)
    tab = jnp.concatenate([a_cols.T, p_cols.T])
    tab = jnp.pad(tab, ((0, 0), (0, 128 - fine))).reshape(2 * per_layer, 1, 128)
    half = fine // 2
    early_chunks = (half - PLANE_ROWS // 2) // CHUNK
    chunks = early_chunks + nx * (PLANE_ROWS // 2 // CHUNK)
    row = p_tiles.shape[1:]
    bf, f32, i32 = jnp.bfloat16, jnp.float32, jnp.int32
    dma = pltpu.SemaphoreType.DMA
    return pl.pallas_call(
        functools.partial(main_kernel, nz, nx, nl, cap, per_layer),
        out_shape=jax.ShapeDtypeStruct((1, nx, size, size), bf),
        in_specs=[anywhere, anywhere, anywhere],
        out_specs=pl.BlockSpec(memory_space=pltpu.VMEM),
        scratch_shapes=[
            pltpu.VMEM((4, 1, 128), i32),
            pltpu.SMEM((4, 1, 128), i32),
            pltpu.VMEM((nl, 1, 128), i32),
            pltpu.SMEM((nl, 1, 128), i32),
            pltpu.VMEM((slot_total, size, size), bf),
            pltpu.VMEM((2, early_chunks + PLANE_ROWS // 2 // CHUNK, CHUNK) + row, bf),
            pltpu.VMEM((ng, cap, size, size), bf),
            pltpu.VMEM((nx, nl, cap, size, size), bf),
            pltpu.VMEM((nl, 1, 128), i32),
            pltpu.VMEM((nl, 1, 128), i32),
            pltpu.SMEM((nl, 1, 128), i32),
            pltpu.VMEM((2, chunks, CHUNK) + row, bf),
            pltpu.VMEM((2, 2, early_chunks, CHUNK) + row, bf),
            pltpu.VMEM((2, early_chunks, CHUNK) + row, bf),
            pltpu.VMEM((nx, 2, 1, 128), i32),
            pltpu.SMEM((nx, 2, 1, 128), i32),
            pltpu.VMEM((fine + 1, 3 * size, size), bf),
            pltpu.VMEM((fine, size, 3 * size), bf),
            pltpu.VMEM((3 * size, 3 * size), f32),
            pltpu.VMEM((3, nx + 2, size, size), f32),
            pltpu.VMEM((2, nx, size, size), bf),
            pltpu.VMEM((6, size, size), bf),
            pltpu.VMEM((2, nx, size, size), bf),
            pltpu.VMEM((6, size, size), bf),
            dma((8,)),
            dma((nx,)), dma((nx,)), dma((2,)),
            dma((2,)), dma((2, chunks)),
            dma((2, 2)), dma((2, 2, PARTS)),
            dma((2,)), dma((2,)),
            dma((3, 4)), dma((3, 2)),
            dma((4,)), dma((4,)),
            dma((8,)), dma((8,)),
        ],
        compiler_params=pltpu.CompilerParams(
            collective_id=0, has_side_effects=True, vmem_limit_bytes=58 * 1024 * 1024
        ),
    )(tab, a_tiles.reshape(slot_total, size, size), p_tiles.reshape((2, early_chunks + PLANE_ROWS // 2 // CHUNK, CHUNK) + row))


def solution(mesh):
    nx = 4
    return jax.shard_map(
        functools.partial(local, nx),
        mesh=mesh,
        in_specs=(
            P("grid", "layer", None, None),
            P("grid", "layer"),
            P("grid", None, None, None),
            P("grid", None),
        ),
        out_specs=P("grid", "layer", None, None),
        check_vma=False,
    )
```
